256 devices in a mesh: ep: 64 (over x, z_lo, y), dp: 4 (over z_hi, core).
Axes of the slice: x: 4, y: 4, z: 8 (z_hi: 2, z_lo: 4; z = z_hi * 4 + z_lo), core: 2. Of those that a mesh axis runs over, the one named last changes fastest.
Arguments:
- hidden_acts: bfloat16 [8192, 2, 2560], P('ep', None, 'dp'), may hold values from -6 to 6
- out_grad: bfloat16 [8192, 3584], P('ep'), may hold values from -6 to 6
- gate_probs: float32 [8192, 2], P('ep'), may hold values from 0.05 to 0.95
- route: int32 [8192, 2], P('ep'), may hold values from 0 to 15, all different within a row; in each aligned block of 128 rows (0 to 127, 128 to 255, ...) at most 24 rows name the same one
- weights: bfloat16 [64, 2560, 896], P('ep', 'dp'), may hold values from -0.09375 to 0.09375
- first_moment: float32 [64, 2560, 896], P('ep', 'dp'), may hold values from -96 to 96
- second_moment: float32 [64, 2560, 896], P('ep', 'dp'), may hold values from 64 to 1024
- old_slot: int32 [16], replicated, may hold values from 0 to 15, each once
- new_slot: int32 [16], replicated, may hold values from 0 to 15, each once
- partner: int32 [16], replicated, may hold values from 0 to 15, as said below
Outputs:
- hidden_grad: bfloat16 [8192, 2, 2560], P('ep', None, 'dp')
- expert_update: float32 [64, 2560, 896], P('ep', 'dp')
The draws below stay inside these ranges and needn't reach their ends.
Inputs may be any that keep to these rules, and one draw needn't show every extreme that they name: `route`: among the 128 rows of one ep index no expert is named by more than 24 rows, a bound that some block reaches; the 2 experts of a row differ. `old_slot`: A permutation of the owners. `new_slot`: A permutation of the owners. partner[partner[e]] = e; exactly 4 pairs of distinct experts, all others their own partner.
All inputs are finite; a program needn't handle non-finite values.
Results may differ from the reference program's by a relative error of at most 0.00105.
The reference program's roundings to bfloat16 on the way (of `scaled` and `expert_w`) count: a program that leaves them out, or rounds other values in their place, can miss the bound.
Values may be sent and summed in bfloat16 or wider, within the bound.
No kernel may reach another device: no remote copies, remote signals or barrier semaphores. Data moves between devices by JAX's collectives and lax.ppermute only.
A program may use at most 128 MiB of HBM per device.

```python
import math
import jax
import jax.numpy as jnp
import numpy as np
from jax import lax

D = 3584
FF = 2560
TOP = 2
TOK_DEV = 128
RUN = 4
EXPERTS = 16
TOKENS = 8192
MOST = 24
N_EP = 64


def draw_partner(key, part):
    key = jax.random.fold_in(key, 7)
    order_ids = jax.random.permutation(key, EXPERTS).astype(jnp.int32)
    pair_count = max(1, EXPERTS // 4)
    positions = jnp.arange(EXPERTS, dtype=jnp.int32)
    mate_pos = jnp.where(positions < 2 * pair_count, positions + 1 - 2 * (positions % 2), positions)
    return jnp.zeros((EXPERTS,), jnp.int32).at[order_ids].set(order_ids[mate_pos])


def levels(key, shape, split, least, high):
    gain, own = 1.0, jax.random.fold_in(key, 6)
    for position, parts in split:
        draws = jnp.exp(jax.random.uniform(jax.random.fold_in(own, position), (parts,), jnp.float32, least / len(split), high / len(split)))
        gain = gain * jnp.repeat(draws, shape[position] // parts).reshape([-1 if axis == position else 1 for axis in range(len(shape))])
    return gain


def assign_block(key, own, number, rows, amount, top, bound, slope):
    order = jax.random.permutation(key, amount)
    packed, ordinary = portions_of(amount, rows * top, bound, slope, True), portions_of(amount, rows * top, bound, slope, False)
    places = jnp.arange(amount)

    def named(tallies, offset_by):
        used = int((tallies > 0).sum())
        fixed = max(1, used // 4)
        passed = fixed + (places - fixed + offset_by * (used - fixed)) % max(1, amount - fixed)
        return jnp.zeros((amount,), jnp.int32).at[order[jnp.where(places < fixed, places, passed)]].set(jnp.asarray(tallies, jnp.int32))

    tallies = jnp.where(number % 4 == 0, named(packed, number // 4), named(ordinary, number - number // 4 - 1))
    mixed = jax.random.permutation(jax.random.fold_in(own, 3), amount)
    giver, receiver = mixed[0:amount // 2 * 2:2], mixed[1:amount // 2 * 2:2]
    slack = jnp.minimum(tallies[giver] - 1, bound - tallies[receiver]) // 2
    slack = jnp.where((giver == order[0]) | (receiver == order[0]) | (tallies[receiver] == 0), 0, jnp.maximum(slack, 0))
    passed = jax.random.randint(jax.random.fold_in(own, 4), (amount // 2,), 0, 1 << 20) % (slack + 1)
    tallies = tallies.at[giver].add(-passed).at[receiver].add(passed)
    items = jnp.searchsorted(jnp.cumsum(tallies), jnp.arange(rows * top), side="right").astype(jnp.int32)
    listing = items.reshape(top, rows).T
    listing = listing[jax.random.permutation(jax.random.fold_in(own, 1), rows)]
    offset_by = jax.random.randint(jax.random.fold_in(own, 2), (rows, 1), 0, top)
    return jnp.take_along_axis(listing, (jnp.arange(top)[None, :] + offset_by) % top, axis=1)


def portions_of(number_of, total, limit, lean, full):
    portions = [(1 << 20) // math.isqrt(standing ** lean) + 1 for standing in range(1, number_of + 1)]
    largest = limit if full else min(limit, max(-(-total // number_of), total * portions[0] // sum(portions)))
    least = 1 if total - largest >= number_of - 1 else 0
    given, rest = [largest] + [least] * (number_of - 1), total - largest - least * (number_of - 1)
    while rest > 0:
        free = [i for i in range(1, number_of) if given[i] < largest] or [i for i in range(1, number_of) if given[i] < limit]
        pool, budget = sum([portions[i] for i in free]), rest
        for i in free:
            addition = min(limit - given[i], max(1, budget * portions[i] // pool), rest)
            given[i] = given[i] + addition
            rest = rest - addition
    return np.array(given)


def gaussian(own_key, dims, deviation, bound, pieces=(), kind=jnp.bfloat16):
    result = jax.random.normal(own_key, dims, jnp.float32) * deviation
    if len(pieces) > 0:
        result = levels(own_key, dims, pieces, -0.22, 0.18) * result
    return jnp.clip(result, min=-bound, max=bound).astype(kind)


def setup_inputs(seed: int = 0) -> dict:
    streams_of = jax.random.split(jax.random.key(seed), 11)
    hidden_acts = gaussian(streams_of[0], (TOKENS, TOP, FF), 1.0, 6.0, ((0, 64), (2, 4)))
    out_grad = gaussian(streams_of[1], (TOKENS, D), 1.0, 6.0, ((0, 64),))
    gate_probs = jnp.clip(jnp.exp(math.log(0.95) - 2.944439 * jax.random.uniform(streams_of[2], (TOKENS, TOP), jnp.float32) ** levels(streams_of[2], (TOKENS, TOP), ((0, 64),), -0.2, 0.2)), 0.05, 0.95)
    route_keys = jax.random.split(jax.random.fold_in(streams_of[3], 1), TOKENS // TOK_DEV)
    route_turns = jax.random.permutation(jax.random.fold_in(streams_of[3], 3), TOKENS // TOK_DEV)
    route = jax.vmap(lambda own, number: assign_block(jax.random.fold_in(streams_of[3], 2), own, number, TOK_DEV, EXPERTS, TOP, MOST, 2))(route_keys, route_turns).reshape((TOKENS, TOP))
    weights = gaussian(streams_of[4], (N_EP, FF, D // RUN), D ** -0.5, 0.09375, ((0, 64), (1, 4)))
    first_moment = gaussian(streams_of[5], (N_EP, FF, D // RUN), 16.0, 96.0, ((0, 64), (1, 4)), jnp.float32)
    second_moment = jnp.clip(jnp.exp(math.log(1024.0) - 2.7725887 * jax.random.uniform(streams_of[6], (N_EP, FF, D // RUN), jnp.float32) ** levels(streams_of[6], (N_EP, FF, D // RUN), ((0, 64), (1, 4)), -0.2, 0.2)), 64.0, 1024.0)
    old_slot = jax.random.permutation(streams_of[7], EXPERTS).astype(jnp.int32)
    new_slot = jax.random.permutation(streams_of[8], EXPERTS).astype(jnp.int32)
    partner = draw_partner(jax.random.fold_in(streams_of[10], 71), 0)
    return dict(hidden_acts=hidden_acts, out_grad=out_grad, gate_probs=gate_probs, route=route, weights=weights, first_moment=first_moment, second_moment=second_moment, old_slot=old_slot, new_slot=new_slot, partner=partner)


beta_one = 0.9
beta_two = 0.95
decay = 0.1
epsilon = 1e-08
bias_one = 1.0 - (0.9 ** 50) ** 2
bias_two = 1.0 - (0.95 ** 50) ** 2

def to_full(slab_arr):
    owners = slab_arr.shape[0] // RUN
    return slab_arr.reshape(owners, RUN, FF, D // RUN).transpose(0, 2, 1, 3).reshape(owners, FF, D)

def from_full(full_arr):
    owners = full_arr.shape[0]
    return full_arr.reshape(owners, FF, RUN, D // RUN).transpose(0, 2, 1, 3).reshape(owners * RUN, FF, D // RUN)

def reference(hidden_acts, out_grad, gate_probs, route, weights, first_moment, second_moment, old_slot, new_slot, partner):
    row_count = route.shape[0] * route.shape[1]
    scaled = (gate_probs[:, :, None] * out_grad.astype(jnp.float32)[:, None, :]).astype(jnp.bfloat16).reshape(row_count, D)
    scaled_pad = jnp.concatenate([scaled, jnp.zeros((1, D), jnp.bfloat16)], axis=0)
    acts_pad = jnp.concatenate([hidden_acts.reshape(row_count, FF), jnp.zeros((1, FF), jnp.bfloat16)], axis=0)
    flat_route = route.reshape(row_count)
    expert_w = to_full(weights)[old_slot]
    live_rows = N_EP * MOST

    def per_expert(expert_id):
        row_ids = jnp.nonzero(flat_route == expert_id, size=live_rows, fill_value=row_count)[0].astype(jnp.int32)
        h_rows = acts_pad[row_ids]
        c_rows = scaled_pad[row_ids]
        grad_part = jnp.dot(h_rows.T, c_rows, preferred_element_type=jnp.float32)
        back_part = jnp.dot(c_rows, expert_w[expert_id].T, preferred_element_type=jnp.float32)
        return (grad_part, back_part, row_ids)
    all_grads, all_backs, all_rows = lax.map(per_expert, jnp.arange(old_slot.shape[0], dtype=jnp.int32))
    hidden_grad = jnp.zeros((row_count + 1, FF), jnp.float32).at[all_rows.reshape(-1)].set(all_backs.reshape(-1, FF))
    hidden_grad = hidden_grad[:row_count].astype(jnp.bfloat16).reshape(route.shape[0], route.shape[1], FF)
    paired = partner != jnp.arange(partner.shape[0], dtype=jnp.int32)
    total_grad = all_grads + jnp.where(paired[:, None, None], all_grads[partner], jnp.float32(0.0))
    moment_one = to_full(first_moment)[old_slot]
    moment_two = to_full(second_moment)[old_slot]
    m_new = beta_one * moment_one + (1.0 - beta_one) * total_grad
    v_new = beta_two * moment_two + (1.0 - beta_two) * total_grad * total_grad
    direction = m_new / bias_one / (jnp.sqrt(v_new / bias_two) + epsilon) + decay * expert_w.astype(jnp.float32)
    placed = jnp.zeros_like(direction).at[new_slot].set(direction)
    return (hidden_grad, from_full(placed))
```

```python
import jax
import jax.numpy as jnp
from jax import lax
from jax.experimental import pallas as pl
from jax.experimental.pallas import tpu as pltpu
from jax.sharding import PartitionSpec as P

beta_one = 0.9
beta_two = 0.95
decay = 0.1
epsilon = 1e-08
bias_one = 1.0 - (0.9**50) ** 2
bias_two = 1.0 - (0.95**50) ** 2

RUN = 4
GROUPS = 16
CAP = 24
ROWS = GROUPS * CAP
SCALE = 2048.0
SAME_Y = [[g * RUN + y for g in range(GROUPS)] for y in range(RUN)]
SAME_RUN = [[g * RUN + y for y in range(RUN)] for g in range(GROUPS)]
OTHER_CORE = [(0, 1), (1, 0), (2, 3), (3, 2)]
MB = 1024 * 1024


def contract(a, b, dims):
    return lax.dot_general(a, b, ((dims[0], dims[1]), ((), ())), preferred_element_type=jnp.float32)


def order_of(index, tokens):
    return 2 * (index % tokens) + index // tokens


def choose(row, col, want):
    count = row.shape[1]
    tokens = count // 2
    lane = order_of(lax.broadcasted_iota(jnp.int32, (count, count), 1), tokens)
    line = order_of(lax.broadcasted_iota(jnp.int32, (count, count), 0), tokens)
    ahead = jnp.where((row == col) & (line < lane), 1.0, 0.0)
    position = jnp.sum(ahead, axis=0, keepdims=True)
    place = (lax.broadcasted_iota(jnp.int32, (want.shape[0], 1), 0) % CAP).astype(jnp.float32)
    return (row == want) & (position == place)


def send_h_kernel(row_ref, col_ref, want_ref, acts_ref, out_ref):
    width = acts_ref.shape[1]
    for kind in range(2):
        sel = choose(row_ref[0], col_ref[0], want_ref[kind])
        rows = contract(jnp.where(sel, 1.0, 0.0).astype(jnp.bfloat16), acts_ref[...], ((1,), (0,)))
        out_ref[:, kind * width : (kind + 1) * width] = rows.astype(jnp.bfloat16)


def send_c_kernel(core_ref, row_ref, col_ref, gate_ref, want_ref, grad_ref, out_ref):
    sel = choose(row_ref[0], col_ref[0], want_ref[0])
    gate = jnp.sum(jnp.where(sel, gate_ref[0], 0.0), axis=1, keepdims=True)
    sel = jnp.where(sel, 1.0, 0.0)
    tokens = sel.shape[1] // 2
    sel = (sel[:, :tokens] + sel[:, tokens:]).astype(jnp.bfloat16)
    rows = contract(sel, grad_ref[0], ((1,), (0,)))
    out_ref[...] = (gate * rows).astype(jnp.bfloat16)


def back_kernel(core_ref, own_ref, mate_ref, w_ref, out_ref):
    mine = pl.program_id(0) // 2 == core_ref[0]

    @pl.when(mine)
    def _():
        out_ref[0] = contract(own_ref[...], w_ref[...], ((1,), (1,)))

    @pl.when(jnp.logical_not(mine))
    def _():
        out_ref[0] = contract(mate_ref[...], w_ref[...], ((1,), (1,)))


def update_kernel(
    core_ref, h_own_ref, h_extra_ref, own_ref, mate_ref, w_ref, m_ref, v_ref, out_ref
):
    core = core_ref[0]
    width = w_ref.shape[1]
    total = jnp.zeros(w_ref.shape, jnp.float32)
    for c_ref, base in ((own_ref, 2 * core), (mate_ref, 2 - 2 * core)):
        for kind, h_ref in enumerate((h_own_ref, h_extra_ref)):
            for j in range(2):
                part = 2 * kind + j
                total += contract(
                    h_ref[base + j], c_ref[:, part * width : (part + 1) * width], ((0,), (0,))
                )
    m_new = beta_one * m_ref[...] + (1.0 - beta_one) * total
    v_new = beta_two * v_ref[...] + (1.0 - beta_two) * total * total
    direction = m_new / bias_one / (jnp.sqrt(v_new / bias_two) + epsilon)
    direction = direction + decay * w_ref[...].astype(jnp.float32)
    out_ref[...] = SCALE * direction


def take_kernel(row_ref, col_ref, want_ref, back_ref, out_ref):
    sel = jnp.where(choose(row_ref[0], col_ref[0], want_ref[0]), 1.0, 0.0).astype(jnp.bfloat16)
    out_ref[...] = contract(sel, back_ref[...], ((0,), (0,))).astype(jnp.bfloat16)


def params(limit):
    return pltpu.CompilerParams(vmem_limit_bytes=limit * MB)


def whole(shape):
    return pl.BlockSpec(shape, lambda *_: (0,) * len(shape))


def local(
    hidden_acts,
    out_grad,
    gate_probs,
    route,
    weights,
    first_moment,
    second_moment,
    old_slot,
    new_slot,
    partner,
):
    tokens, top, hidden = hidden_acts.shape
    count = tokens * top
    width = weights.shape[2]
    core = (lax.axis_index("dp") % 2).astype(jnp.int32).reshape(1)

    numbers = jnp.arange(GROUPS, dtype=jnp.int32)
    held = old_slot[None, :] == numbers[:, None]
    own = jnp.sum(jnp.where(held, numbers[None, :], 0), axis=1)
    mate = jnp.sum(jnp.where(held, partner[None, :], 0), axis=1)
    mate = jnp.where(mate == own, -1, mate)
    want = jnp.stack([own, mate]).astype(jnp.float32)
    want = jnp.broadcast_to(want[:, :, None], (2, GROUPS, CAP)).reshape(2, ROWS, 1)
    source = jnp.sum(
        jnp.where(new_slot[None, :] == numbers[:, None], old_slot[None, :], 0), axis=1
    )

    about = jnp.concatenate([route.astype(jnp.float32).T, gate_probs.T], axis=0)
    about = lax.all_gather(about, "ep", axis_index_groups=SAME_RUN, axis=0, tiled=False)
    rows = about[:, :top].reshape(RUN, 1, count)
    gates = about[:, top:].reshape(RUN, 1, count)
    quarters = out_grad.reshape(tokens, RUN, width).transpose(1, 0, 2)
    quarters = lax.all_to_all(quarters, "ep", 0, 0, axis_index_groups=SAME_RUN, tiled=True)

    own_row = route.astype(jnp.float32).T.reshape(1, 1, count)
    own_col = own_row.reshape(1, count, 1)
    acts = hidden_acts.transpose(1, 0, 2).reshape(count, hidden)
    send_h = pl.pallas_call(
        send_h_kernel,
        out_shape=jax.ShapeDtypeStruct((ROWS, 2 * hidden), jnp.bfloat16),
        compiler_params=params(32),
        name="send_h",
    )(own_row, own_col, want, acts)
    got_h = lax.all_to_all(send_h, "ep", 0, 0, axis_index_groups=SAME_Y, tiled=True)
    all_h = lax.all_gather(got_h, "ep", axis_index_groups=SAME_RUN, axis=0, tiled=False)

    send_c = pl.pallas_call(
        send_c_kernel,
        grid_spec=pltpu.PrefetchScalarGridSpec(
            num_scalar_prefetch=1,
            grid=(2, 2),
            in_specs=[
                pl.BlockSpec((1, 1, count), lambda k, j, c: (2 * c[0] + j, 0, 0)),
                pl.BlockSpec((1, count, 1), lambda k, j, c: (2 * c[0] + j, 0, 0)),
                pl.BlockSpec((1, 1, count), lambda k, j, c: (2 * c[0] + j, 0, 0)),
                pl.BlockSpec((1, ROWS, 1), lambda k, j, c: (k, 0, 0)),
                pl.BlockSpec((1, tokens, width), lambda k, j, c: (2 * c[0] + j, 0, 0)),
            ],
            out_specs=pl.BlockSpec((ROWS, width), lambda k, j, c: (0, 2 * k + j)),
        ),
        out_shape=jax.ShapeDtypeStruct((ROWS, 4 * width), jnp.bfloat16),
        compiler_params=params(32),
        name="send_c",
    )(core, rows, rows.reshape(RUN, count, 1), gates, want, quarters)
    got_c = lax.all_to_all(send_c, "ep", 0, 0, axis_index_groups=SAME_Y, tiled=True)
    mate_c = lax.ppermute(got_c, "dp", OTHER_CORE)

    weight = weights[0]
    partial_back = pl.pallas_call(
        back_kernel,
        grid_spec=pltpu.PrefetchScalarGridSpec(
            num_scalar_prefetch=1,
            grid=(RUN,),
            in_specs=[
                pl.BlockSpec((ROWS, width), lambda s, c: (0, s % 2)),
                pl.BlockSpec((ROWS, width), lambda s, c: (0, s % 2)),
                whole((hidden, width)),
            ],
            out_specs=pl.BlockSpec((1, ROWS, hidden), lambda s, c: (s, 0, 0)),
        ),
        out_shape=jax.ShapeDtypeStruct((RUN, ROWS, hidden), jnp.float32),
        compiler_params=params(32),
        name="back",
    )(core, got_c, mate_c, weight)
    summed = lax.psum_scatter(
        partial_back, "ep", scatter_dimension=0, axis_index_groups=SAME_RUN, tiled=False
    )
    back = lax.all_to_all(
        summed.astype(jnp.bfloat16), "ep", 0, 0, axis_index_groups=SAME_Y, tiled=True
    )
    hidden_out = pl.pallas_call(
        take_kernel,
        out_shape=jax.ShapeDtypeStruct((count, hidden), jnp.bfloat16),
        compiler_params=params(32),
        name="take",
    )(own_row, own_col, want, back)
    hidden_out = hidden_out.reshape(top, tokens, hidden).transpose(1, 0, 2)

    block = 128
    steps = hidden // block
    update = pl.pallas_call(
        update_kernel,
        grid_spec=pltpu.PrefetchScalarGridSpec(
            num_scalar_prefetch=1,
            grid=(steps,),
            in_specs=[
                pl.BlockSpec((RUN, ROWS, block), lambda i, c: (0, 0, i)),
                pl.BlockSpec((RUN, ROWS, block), lambda i, c: (0, 0, steps + i)),
                whole((ROWS, 4 * width)),
                whole((ROWS, 4 * width)),
                pl.BlockSpec((block, width), lambda i, c: (i, 0)),
                pl.BlockSpec((block, width), lambda i, c: (i, 0)),
                pl.BlockSpec((block, width), lambda i, c: (i, 0)),
            ],
            out_specs=pl.BlockSpec((block, width), lambda i, c: (i, 0)),
        ),
        out_shape=jax.ShapeDtypeStruct((hidden, width), jnp.float32),
        compiler_params=params(48),
        name="update",
    )(core, all_h, all_h, got_c, mate_c, weight, first_moment[0], second_moment[0])

    spread = update.astype(jnp.float16).reshape(GROUPS, hidden // GROUPS, width)
    spread = lax.all_to_all(spread, "ep", 0, 0, axis_index_groups=SAME_Y, tiled=True)
    placed = lax.all_to_all(spread[source], "ep", 0, 0, axis_index_groups=SAME_Y, tiled=True)
    placed = placed.reshape(1, hidden, width).astype(jnp.float32) * (1.0 / SCALE)
    return (hidden_out, placed)


def solution(mesh):
    return jax.shard_map(
        local,
        mesh=mesh,
        in_specs=(
            P("ep", None, "dp"),
            P("ep", None),
            P("ep", None),
            P("ep", None),
            P("ep", "dp", None),
            P("ep", "dp", None),
            P("ep", "dp", None),
            P(),
            P(),
            P(),
        ),
        out_specs=(P("ep", None, "dp"), P("ep", "dp", None)),
        check_vma=False,
    )
```

```python
import jax
import jax.numpy as jnp
from jax import lax
from jax.experimental import pallas as pl
from jax.experimental.pallas import tpu as pltpu
from jax.sharding import PartitionSpec as P

beta_one = 0.9
beta_two = 0.95
decay = 0.1
epsilon = 1e-08
bias_one = 1.0 - (0.9**50) ** 2
bias_two = 1.0 - (0.95**50) ** 2

RUN = 4
GROUPS = 16
CAP = 24
ROWS = GROUPS * CAP
SCALE = 2048.0
SAME_Y = [[g * RUN + y for g in range(GROUPS)] for y in range(RUN)]
SAME_RUN = [[g * RUN + y for y in range(RUN)] for g in range(GROUPS)]
OTHER_CORE = [(0, 1), (1, 0), (2, 3), (3, 2)]
GRID = 4
SHIFTS = [(0, 0), (2, 2), (1, 2), (3, 2), (2, 1), (2, 3), (1, 1), (3, 3)]
SHIFTS += [(1, 3), (3, 1), (0, 2), (2, 0), (0, 1), (0, 3), (1, 0), (3, 0)]
HALF = GROUPS // 2
LANES = 128
MB = 1024 * 1024


def contract(a, b, dims):
    return lax.dot_general(a, b, ((dims[0], dims[1]), ((), ())), preferred_element_type=jnp.float32)


def order_of(index, tokens):
    return 2 * (index % tokens) + index // tokens


def choose(row, col, want):
    count = row.shape[1]
    tokens = count // 2
    lane = order_of(lax.broadcasted_iota(jnp.int32, (count, count), 1), tokens)
    line = order_of(lax.broadcasted_iota(jnp.int32, (count, count), 0), tokens)
    ahead = jnp.where((row == col) & (line < lane), 1.0, 0.0)
    position = jnp.sum(ahead, axis=0, keepdims=True)
    place = (lax.broadcasted_iota(jnp.int32, (want.shape[0], 1), 0) % CAP).astype(jnp.float32)
    return (row == want) & (position == place)


def along_y(step):
    return [(i, i // RUN * RUN + (i + step) % RUN) for i in range(GROUPS * RUN)]


def nearest(step_x, step_z):
    pairs = []
    for i in range(GROUPS * RUN):
        x, z_low, y = i // (GRID * RUN), i // RUN % GRID, i % RUN
        for d in range(4):
            z = d // 2 * GRID + z_low
            step = (2 if z % 2 == 0 else -2) if step_z == 2 else (-1 if step_z == 3 else step_z)
            to_z = (z + step) % (2 * GRID)
            to = ((x + step_x) % GRID * GRID + to_z % GRID) * RUN + y
            pairs.append((i * 4 + d, to * 4 + to_z // GRID * 2 + d % 2))
    return pairs


def pack_kernel(y_ref, grad_ref, about_ref, *out_refs):
    width = grad_ref.shape[1] // RUN
    tokens = grad_ref.shape[0]
    about = about_ref[...]
    lane = lax.broadcasted_iota(jnp.int32, (tokens, LANES), 1)
    block = jnp.zeros((tokens, LANES), jnp.float32)
    place = 0
    for k in range(4):
        rest = about[:, k : k + 1]
        for _ in range(1 if k < 2 else 3):
            piece = rest.astype(jnp.bfloat16).astype(jnp.float32)
            block = jnp.where(lane == place, piece, block)
            rest = rest - piece
            place += 1
    for step, out_ref in enumerate(out_refs):
        quarter = (y_ref[0] + step) % RUN
        start = pl.multiple_of(quarter * width, LANES)
        out_ref[:, :width] = grad_ref[:, pl.ds(start, width)]
        out_ref[:, width:] = block.astype(jnp.bfloat16)


def send_h_kernel(row_ref, col_ref, want_ref, acts_ref, own_ref, extra_ref):
    for kind, out_ref in enumerate((own_ref, extra_ref)):
        sel = choose(row_ref[0], col_ref[0], want_ref[kind])
        rows = contract(jnp.where(sel, 1.0, 0.0).astype(jnp.bfloat16), acts_ref[...], ((1,), (0,)))
        out_ref[...] = rows.astype(jnp.bfloat16)


def send_c_kernel(core_ref, want_ref, packed_ref, *out_refs):
    tokens = packed_ref.shape[1]
    width = packed_ref.shape[2] - LANES
    block = packed_ref[0, :, width:]
    eye = lax.broadcasted_iota(jnp.int32, (tokens, tokens), 0) == lax.broadcasted_iota(
        jnp.int32, (tokens, tokens), 1
    )
    lines = contract(block, jnp.where(eye, 1.0, 0.0).astype(jnp.bfloat16), ((0,), (0,)))
    columns = block.astype(jnp.float32)
    row = jnp.concatenate([lines[0:1], lines[1:2]], axis=1)
    col = jnp.concatenate([columns[:, 0:1], columns[:, 1:2]], axis=0)
    gates = [lines[2 + 3 * k : 3 + 3 * k] + lines[3 + 3 * k : 4 + 3 * k] for k in range(2)]
    gates = [gates[k] + lines[4 + 3 * k : 5 + 3 * k] for k in range(2)]
    sel = choose(row, col, want_ref[0])
    gate = jnp.sum(
        jnp.where(sel, jnp.concatenate(gates, axis=1), 0.0), axis=1, keepdims=True
    )
    sel = jnp.where(sel, 1.0, 0.0)
    sel = (sel[:, :tokens] + sel[:, tokens:]).astype(jnp.bfloat16)
    rows = gate * contract(sel, packed_ref[0, :, :width], ((1,), (0,)))
    for i, out_ref in enumerate(out_refs):
        out_ref[...] = rows[i * CAP : (i + 1) * CAP].astype(jnp.bfloat16)


def order_kernel(order_ref, *refs):
    values, out_ref = refs[:-1], refs[-1]
    lane = lax.broadcasted_iota(jnp.int32, (ROWS, ROWS), 1)
    turn = jnp.where(lane == order_ref[...], 1.0, 0.0).astype(jnp.bfloat16)
    out_ref[...] = contract(turn, values[0][...], ((1,), (0,))).astype(jnp.bfloat16)


def unorder_kernel(order_ref, first_ref, second_ref, out_ref):
    lane = lax.broadcasted_iota(jnp.int32, (ROWS, ROWS), 1)
    turn = jnp.where(lane == order_ref[...], 1.0, 0.0).astype(jnp.bfloat16)
    half = ROWS // 2
    out_ref[...] = (
        contract(turn[:half], first_ref[...].astype(jnp.bfloat16), ((0,), (0,)))
        + contract(turn[half:], second_ref[...].astype(jnp.bfloat16), ((0,), (0,)))
    ).astype(jnp.bfloat16)


def back_kernel(core_ref, own_ref, mate_ref, w_ref, out_ref):
    mine = pl.program_id(0) // 2 == core_ref[0]

    @pl.when(mine)
    def _():
        out_ref[0] = contract(own_ref[...], w_ref[...], ((1,), (1,)))

    @pl.when(jnp.logical_not(mine))
    def _():
        out_ref[0] = contract(mate_ref[...], w_ref[...], ((1,), (1,)))


def update_kernel(core_ref, h_own_ref, h_extra_ref, *refs):
    own_refs, mate_refs = refs[0:2], refs[2:4]
    w_ref, m_ref, v_ref, out_ref = refs[4:]
    core = core_ref[0]
    width = w_ref.shape[1]
    half = ROWS // 2
    total = jnp.zeros(w_ref.shape, jnp.float32)
    for c_refs, base in ((own_refs, 2 * core), (mate_refs, 2 - 2 * core)):
        for kind, h_ref in enumerate((h_own_ref, h_extra_ref)):
            for j in range(2):
                part = 2 * kind + j
                for at, c_ref in enumerate(c_refs):
                    total += contract(
                        h_ref[base + j, at * half : (at + 1) * half],
                        c_ref[:, part * width : (part + 1) * width],
                        ((0,), (0,)),
                    )
    m_new = beta_one * m_ref[...] + (1.0 - beta_one) * total
    v_new = beta_two * v_ref[...] + (1.0 - beta_two) * total * total
    direction = m_new / bias_one / (jnp.sqrt(v_new / bias_two) + epsilon)
    direction = direction + decay * w_ref[...].astype(jnp.float32)
    out_ref[...] = SCALE * direction


def take_kernel(row_ref, col_ref, want_ref, back_ref, out_ref):
    sel = jnp.where(choose(row_ref[0], col_ref[0], want_ref[0]), 1.0, 0.0).astype(jnp.bfloat16)
    out_ref[...] = contract(sel, back_ref[...], ((0,), (0,))).astype(jnp.bfloat16)


def params(limit):
    return pltpu.CompilerParams(vmem_limit_bytes=limit * MB)


def whole(shape):
    return pl.BlockSpec(shape, lambda *_: (0,) * len(shape))


def local(
    hidden_acts,
    out_grad,
    gate_probs,
    route,
    weights,
    first_moment,
    second_moment,
    old_slot,
    new_slot,
    partner,
):
    tokens, top, hidden = hidden_acts.shape
    count = tokens * top
    width = weights.shape[2]
    index = lax.axis_index("ep").astype(jnp.int32)
    y = index % RUN
    core = (lax.axis_index("dp") % 2).astype(jnp.int32)
    cores = core.reshape(1)

    numbers = jnp.arange(GROUPS, dtype=jnp.int32)
    held = old_slot[None, :] == numbers[:, None]
    own = jnp.sum(jnp.where(held, numbers[None, :], 0), axis=1)
    mate = jnp.sum(jnp.where(held, partner[None, :], 0), axis=1)
    mate = jnp.where(mate == own, -1, mate)
    want = jnp.stack([own, mate]).astype(jnp.float32)
    steps = jnp.array(SHIFTS, jnp.int32)
    x, z = index // (GRID * RUN), index // RUN % GRID
    to = (x + steps[:, 0]) % GRID * GRID + (z + steps[:, 1]) % GRID
    by = (x - steps[:, 0]) % GRID * GRID + (z - steps[:, 1]) % GRID
    want_to = jnp.sum(jnp.where(to[:, None] == numbers[None, :], want[:, None, :], 0.0), axis=2)
    want = jnp.broadcast_to(want[:, :, None], (2, GROUPS, CAP)).reshape(2, ROWS, 1)
    want_to = jnp.broadcast_to(want_to[:, :, None], (2, GROUPS, CAP)).reshape(2, ROWS, 1)
    order = (by[:, None] * CAP + jnp.arange(CAP, dtype=jnp.int32)[None, :]).reshape(ROWS, 1)
    source = jnp.sum(
        jnp.where(new_slot[None, :] == numbers[:, None], old_slot[None, :], 0), axis=1
    )

    routes = route.astype(jnp.float32)
    packed = pl.pallas_call(
        pack_kernel,
        grid_spec=pltpu.PrefetchScalarGridSpec(
            num_scalar_prefetch=1,
            grid=(1,),
            in_specs=[whole((tokens, RUN * width)), whole((tokens, 2 * top))],
            out_specs=[whole((tokens, width + LANES))] * RUN,
        ),
        out_shape=[jax.ShapeDtypeStruct((tokens, width + LANES), jnp.bfloat16)] * RUN,
        compiler_params=params(16),
        name="pack",
    )(y.reshape(1), out_grad, jnp.concatenate([routes, gate_probs], axis=1))
    packed = [packed[0]] + [lax.ppermute(packed[s], "ep", along_y(s)) for s in range(1, RUN)]
    packed = jnp.stack(packed)

    own_row = routes.T.reshape(1, 1, count)
    own_col = own_row.reshape(1, count, 1)
    acts = hidden_acts.transpose(1, 0, 2).reshape(count, hidden)
    sent_h = pl.pallas_call(
        send_h_kernel,
        out_shape=[jax.ShapeDtypeStruct((ROWS, hidden), jnp.bfloat16)] * 2,
        compiler_params=params(16),
        name="send_h",
    )(own_row, own_col, want, acts)
    all_h = []
    for kind in range(2):
        got = lax.all_to_all(sent_h[kind], "ep", 0, 0, axis_index_groups=SAME_Y, tiled=True)
        got = pl.pallas_call(
            order_kernel,
            out_shape=jax.ShapeDtypeStruct((ROWS, hidden), jnp.bfloat16),
            compiler_params=params(16),
            name="order_h",
        )(order, got)
        all_h.append(
            lax.all_gather(got, "ep", axis_index_groups=SAME_RUN, axis=0, tiled=False)
        )

    send_c = pl.pallas_call(
        send_c_kernel,
        grid_spec=pltpu.PrefetchScalarGridSpec(
            num_scalar_prefetch=1,
            grid=(2, 2),
            in_specs=[
                pl.BlockSpec((1, ROWS, 1), lambda k, j, c: (k, 0, 0)),
                pl.BlockSpec(
                    (1, tokens, width + LANES),
                    lambda k, j, c: ((c[1] + 2 * RUN - 2 * c[0] - j) % RUN, 0, 0),
                ),
            ],
            out_specs=[pl.BlockSpec((CAP, width), lambda k, j, c: (0, 2 * k + j))] * GROUPS,
        ),
        out_shape=[jax.ShapeDtypeStruct((CAP, 4 * width), jnp.bfloat16)] * GROUPS,
        compiler_params=params(24),
        name="send_c",
    )(jnp.stack([core, y]), want_to, packed)
    got_c = [send_c[0]]
    for step, block in zip(SHIFTS[1:], send_c[1:], strict=True):
        got_c.append(lax.ppermute(block, ("ep", "dp"), nearest(*step)))
    got_c = [jnp.concatenate(got_c[:HALF]), jnp.concatenate(got_c[HALF:])]
    mate_c = [lax.ppermute(part, "dp", OTHER_CORE) for part in got_c]

    weight = weights[0]
    half = ROWS // 2
    summed = []
    for at in range(2):
        partial_back = pl.pallas_call(
            back_kernel,
            grid_spec=pltpu.PrefetchScalarGridSpec(
                num_scalar_prefetch=1,
                grid=(RUN,),
                in_specs=[
                    pl.BlockSpec((half, width), lambda s, c: (0, s % 2)),
                    pl.BlockSpec((half, width), lambda s, c: (0, s % 2)),
                    whole((hidden, width)),
                ],
                out_specs=pl.BlockSpec((1, half, hidden), lambda s, c: (s, 0, 0)),
            ),
            out_shape=jax.ShapeDtypeStruct((RUN, half, hidden), jnp.float32),
            compiler_params=params(16),
            name="back",
        )(cores, got_c[at], mate_c[at], weight)
        summed.append(
            lax.psum_scatter(
                partial_back, "ep", scatter_dimension=0, axis_index_groups=SAME_RUN, tiled=False
            )
        )
    back = pl.pallas_call(
        unorder_kernel,
        out_shape=jax.ShapeDtypeStruct((ROWS, hidden), jnp.bfloat16),
        compiler_params=params(16),
        name="unorder",
    )(order, *summed)
    back = lax.all_to_all(back, "ep", 0, 0, axis_index_groups=SAME_Y, tiled=True)
    hidden_out = pl.pallas_call(
        take_kernel,
        out_shape=jax.ShapeDtypeStruct((count, hidden), jnp.bfloat16),
        compiler_params=params(16),
        name="take",
    )(own_row, own_col, want, back)
    hidden_out = hidden_out.reshape(top, tokens, hidden).transpose(1, 0, 2)

    block = 128
    grid = hidden // block
    update = pl.pallas_call(
        update_kernel,
        grid_spec=pltpu.PrefetchScalarGridSpec(
            num_scalar_prefetch=1,
            grid=(grid,),
            in_specs=[pl.BlockSpec((RUN, ROWS, block), lambda i, c: (0, 0, i))] * 2
            + [whole((half, 4 * width))] * 4
            + [pl.BlockSpec((block, width), lambda i, c: (i, 0))] * 3,
            out_specs=pl.BlockSpec((block, width), lambda i, c: (i, 0)),
        ),
        out_shape=jax.ShapeDtypeStruct((hidden, width), jnp.float32),
        compiler_params=params(24),
        name="update",
    )(cores, *all_h, *got_c, *mate_c, weight, first_moment[0], second_moment[0])

    spread = update.astype(jnp.float16).reshape(GROUPS, hidden // GROUPS, width)
    spread = lax.all_to_all(spread, "ep", 0, 0, axis_index_groups=SAME_Y, tiled=True)
    placed = lax.all_to_all(spread[source], "ep", 0, 0, axis_index_groups=SAME_Y, tiled=True)
    placed = placed.reshape(1, hidden, width).astype(jnp.float32) * (1.0 / SCALE)
    return (hidden_out, placed)


def solution(mesh):
    return jax.shard_map(
        local,
        mesh=mesh,
        in_specs=(
            P("ep", None, "dp"),
            P("ep", None),
            P("ep", None),
            P("ep", None),
            P("ep", "dp", None),
            P("ep", "dp", None),
            P("ep", "dp", None),
            P(),
            P(),
            P(),
        ),
        out_specs=(P("ep", None, "dp"), P("ep", "dp", None)),
        check_vma=False,
    )
```

```python
import jax
import jax.numpy as jnp
from jax import lax
from jax.experimental import pallas as pl
from jax.experimental.pallas import tpu as pltpu
from jax.sharding import PartitionSpec as P

beta_one = 0.9
beta_two = 0.95
decay = 0.1
epsilon = 1e-08
bias_one = 1.0 - (0.9**50) ** 2
bias_two = 1.0 - (0.95**50) ** 2

RUN = 4
GROUPS = 16
CAP = 24
ROWS = GROUPS * CAP
PAIR = 2 * CAP
SCALE = 2048.0
SAME_Y = [[g * RUN + y for g in range(GROUPS)] for y in range(RUN)]
SAME_RUN = [[g * RUN + y for y in range(RUN)] for g in range(GROUPS)]
OTHER_CORE = [(0, 1), (1, 0), (2, 3), (3, 2)]
GRID = 4
SHIFTS = [(0, 0), (2, 2), (1, 2), (3, 2), (2, 1), (2, 3), (1, 1), (3, 3)]
SHIFTS += [(1, 3), (3, 1), (0, 2), (2, 0), (0, 1), (0, 3), (1, 0), (3, 0)]
HALF = GROUPS // 2
LANES = 128
MB = 1024 * 1024


def contract(a, b, dims):
    return lax.dot_general(a, b, ((dims[0], dims[1]), ((), ())), preferred_element_type=jnp.float32)


def order_of(index, tokens):
    return 2 * (index % tokens) + index // tokens


def choose(row, col, want):
    count = row.shape[1]
    tokens = count // 2
    lane = order_of(lax.broadcasted_iota(jnp.int32, (count, count), 1), tokens)
    line = order_of(lax.broadcasted_iota(jnp.int32, (count, count), 0), tokens)
    ahead = jnp.where((row == col) & (line < lane), 1.0, 0.0)
    position = jnp.sum(ahead, axis=0, keepdims=True)
    place = (lax.broadcasted_iota(jnp.int32, (want.shape[0], 1), 0) % CAP).astype(jnp.float32)
    return (row == want) & (position == place)


def along_y(step):
    return [(i, i // RUN * RUN + (i + step) % RUN) for i in range(GROUPS * RUN)]


def nearest(step_x, step_z):
    pairs = []
    for i in range(GROUPS * RUN):
        x, z_low, y = i // (GRID * RUN), i // RUN % GRID, i % RUN
        for d in range(4):
            z = d // 2 * GRID + z_low
            step = (2 if z % 2 == 0 else -2) if step_z == 2 else (-1 if step_z == 3 else step_z)
            to_z = (z + step) % (2 * GRID)
            to = ((x + step_x) % GRID * GRID + to_z % GRID) * RUN + y
            pairs.append((i * 4 + d, to * 4 + to_z // GRID * 2 + d % 2))
    return pairs


def pack_kernel(y_ref, grad_ref, about_ref, *out_refs):
    width = grad_ref.shape[1] // RUN
    tokens = grad_ref.shape[0]
    about = about_ref[...]
    lane = lax.broadcasted_iota(jnp.int32, (tokens, LANES), 1)
    block = jnp.zeros((tokens, LANES), jnp.float32)
    place = 0
    for k in range(4):
        rest = about[:, k : k + 1]
        for _ in range(1 if k < 2 else 3):
            piece = rest.astype(jnp.bfloat16).astype(jnp.float32)
            block = jnp.where(lane == place, piece, block)
            rest = rest - piece
            place += 1
    for step, out_ref in enumerate(out_refs):
        quarter = (y_ref[0] + step) % RUN
        start = pl.multiple_of(quarter * width, LANES)
        out_ref[:, :width] = grad_ref[:, pl.ds(start, width)]
        out_ref[:, width:] = block.astype(jnp.bfloat16)


def send_h_kernel(row_ref, col_ref, want_ref, acts_ref, out_ref):
    sel = jnp.where(choose(row_ref[0], col_ref[0], want_ref[...]), 1.0, 0.0).astype(jnp.bfloat16)
    out_ref[...] = contract(sel, acts_ref[...], ((1,), (0,))).astype(jnp.bfloat16)


def send_c_kernel(core_ref, want_ref, packed_ref, *out_refs):
    tokens = packed_ref.shape[1]
    width = packed_ref.shape[2] - LANES
    block = packed_ref[0, :, width:]
    eye = lax.broadcasted_iota(jnp.int32, (tokens, tokens), 0) == lax.broadcasted_iota(
        jnp.int32, (tokens, tokens), 1
    )
    lines = contract(block, jnp.where(eye, 1.0, 0.0).astype(jnp.bfloat16), ((0,), (0,)))
    columns = block.astype(jnp.float32)
    row = jnp.concatenate([lines[0:1], lines[1:2]], axis=1)
    col = jnp.concatenate([columns[:, 0:1], columns[:, 1:2]], axis=0)
    gates = [lines[2 + 3 * k : 3 + 3 * k] + lines[3 + 3 * k : 4 + 3 * k] for k in range(2)]
    gates = [gates[k] + lines[4 + 3 * k : 5 + 3 * k] for k in range(2)]
    sel = choose(row, col, want_ref[...])
    gate = jnp.sum(
        jnp.where(sel, jnp.concatenate(gates, axis=1), 0.0), axis=1, keepdims=True
    )
    sel = jnp.where(sel, 1.0, 0.0)
    sel = (sel[:, :tokens] + sel[:, tokens:]).astype(jnp.bfloat16)
    rows = (gate * contract(sel, packed_ref[0, :, :width], ((1,), (0,)))).astype(jnp.bfloat16)
    for i, out_ref in enumerate(out_refs):
        out_ref[...] = rows[i * PAIR : (i + 1) * PAIR]


def order_kernel(order_ref, value_ref, out_ref):
    lane = lax.broadcasted_iota(jnp.int32, (2 * ROWS, 2 * ROWS), 1)
    turn = jnp.where(lane == order_ref[...], 1.0, 0.0).astype(jnp.bfloat16)
    out_ref[...] = contract(turn, value_ref[...], ((1,), (0,))).astype(jnp.bfloat16)


def unorder_kernel(order_ref, value_ref, out_ref):
    lane = lax.broadcasted_iota(jnp.int32, (ROWS, ROWS), 1)
    turn = jnp.where(lane == order_ref[...], 1.0, 0.0).astype(jnp.bfloat16)
    out_ref[...] = contract(turn, value_ref[...].astype(jnp.bfloat16), ((0,), (0,))).astype(
        jnp.bfloat16
    )


def join_kernel(*refs):
    for i, ref in enumerate(refs[:-1]):
        refs[-1][i * PAIR : (i + 1) * PAIR] = ref[...]


def back_kernel(core_ref, *refs):
    own_refs, mate_refs = refs[0:2], refs[2:4]
    w_ref, out_ref = refs[4:]
    mine = pl.program_id(0) // 2 == core_ref[0]

    def from_halves(c_refs):
        half = c_refs[0].shape[0]
        for at, c_ref in enumerate(c_refs):
            rows = contract(c_ref[...], w_ref[...], ((1,), (1,)))
            for i in range(half // PAIR):
                start = (at * half // PAIR + i) * CAP
                out_ref[0, start : start + CAP] = rows[i * PAIR : i * PAIR + CAP]

    @pl.when(mine)
    def _():
        from_halves(own_refs)

    @pl.when(jnp.logical_not(mine))
    def _():
        from_halves(mate_refs)


def update_kernel(core_ref, h_ref, *refs):
    own_refs, mate_refs = refs[0:2], refs[2:4]
    w_ref, m_ref, v_ref, out_ref = refs[4:]
    core = core_ref[0]
    width = w_ref.shape[1]
    half = own_refs[0].shape[0]
    total = jnp.zeros(w_ref.shape, jnp.float32)
    for c_refs, base in ((own_refs, 2 * core), (mate_refs, 2 - 2 * core)):
        for j in range(2):
            for at, c_ref in enumerate(c_refs):
                total += contract(
                    h_ref[base + j, at * half : (at + 1) * half],
                    c_ref[:, j * width : (j + 1) * width],
                    ((0,), (0,)),
                )
    m_new = beta_one * m_ref[...] + (1.0 - beta_one) * total
    v_new = beta_two * v_ref[...] + (1.0 - beta_two) * total * total
    direction = m_new / bias_one / (jnp.sqrt(v_new / bias_two) + epsilon)
    direction = direction + decay * w_ref[...].astype(jnp.float32)
    out_ref[...] = SCALE * direction


def take_kernel(row_ref, col_ref, want_ref, back_ref, out_ref):
    sel = jnp.where(choose(row_ref[0], col_ref[0], want_ref[...]), 1.0, 0.0).astype(jnp.bfloat16)
    out_ref[...] = contract(sel, back_ref[...], ((0,), (0,))).astype(jnp.bfloat16)


def params(limit):
    return pltpu.CompilerParams(vmem_limit_bytes=limit * MB)


def whole(shape):
    return pl.BlockSpec(shape, lambda *_: (0,) * len(shape))


def local(
    hidden_acts,
    out_grad,
    gate_probs,
    route,
    weights,
    first_moment,
    second_moment,
    old_slot,
    new_slot,
    partner,
):
    tokens, top, hidden = hidden_acts.shape
    count = tokens * top
    width = weights.shape[2]
    index = lax.axis_index("ep").astype(jnp.int32)
    y = index % RUN
    core = (lax.axis_index("dp") % 2).astype(jnp.int32)
    cores = core.reshape(1)

    numbers = jnp.arange(GROUPS, dtype=jnp.int32)
    held = old_slot[None, :] == numbers[:, None]
    own = jnp.sum(jnp.where(held, numbers[None, :], 0), axis=1)
    mate = jnp.sum(jnp.where(held, partner[None, :], 0), axis=1)
    mate = jnp.where(mate == own, -1, mate)
    want = jnp.stack([own, mate]).astype(jnp.float32)
    steps = jnp.array(SHIFTS, jnp.int32)
    x, z = index // (GRID * RUN), index // RUN % GRID
    to = (x + steps[:, 0]) % GRID * GRID + (z + steps[:, 1]) % GRID
    by = (x - steps[:, 0]) % GRID * GRID + (z - steps[:, 1]) % GRID
    want_to = jnp.sum(jnp.where(to[:, None] == numbers[None, :], want[:, None, :], 0.0), axis=2)
    want_own = jnp.broadcast_to(want[0][:, None], (GROUPS, CAP)).reshape(ROWS, 1)

    def spread_rows(values):
        values = jnp.broadcast_to(values.T[:, :, None], (GROUPS, 2, CAP))
        return values.reshape(2 * ROWS, 1)

    want, want_to = spread_rows(want), spread_rows(want_to)
    order_own = (by[:, None] * CAP + jnp.arange(CAP, dtype=jnp.int32)[None, :]).reshape(ROWS, 1)
    order = (by[:, None] * PAIR + jnp.arange(PAIR, dtype=jnp.int32)[None, :]).reshape(2 * ROWS, 1)
    source = jnp.sum(
        jnp.where(new_slot[None, :] == numbers[:, None], old_slot[None, :], 0), axis=1
    )

    routes = route.astype(jnp.float32)
    packed = pl.pallas_call(
        pack_kernel,
        grid_spec=pltpu.PrefetchScalarGridSpec(
            num_scalar_prefetch=1,
            grid=(1,),
            in_specs=[whole((tokens, RUN * width)), whole((tokens, 2 * top))],
            out_specs=[whole((tokens, width + LANES))] * RUN,
        ),
        out_shape=[jax.ShapeDtypeStruct((tokens, width + LANES), jnp.bfloat16)] * RUN,
        compiler_params=params(16),
        name="pack",
    )(y.reshape(1), out_grad, jnp.concatenate([routes, gate_probs], axis=1))
    packed = [packed[0]] + [lax.ppermute(packed[s], "ep", along_y(s)) for s in range(1, RUN)]
    packed = jnp.stack(packed)

    own_row = routes.T.reshape(1, 1, count)
    own_col = own_row.reshape(1, count, 1)
    acts = hidden_acts.transpose(1, 0, 2).reshape(count, hidden)
    sent_h = pl.pallas_call(
        send_h_kernel,
        out_shape=jax.ShapeDtypeStruct((2 * ROWS, hidden), jnp.bfloat16),
        compiler_params=params(16),
        name="send_h",
    )(own_row, own_col, want, acts)
    got_h = lax.all_to_all(sent_h, "ep", 0, 0, axis_index_groups=SAME_Y, tiled=True)

    send_c = pl.pallas_call(
        send_c_kernel,
        grid_spec=pltpu.PrefetchScalarGridSpec(
            num_scalar_prefetch=1,
            grid=(2,),
            in_specs=[
                whole((2 * ROWS, 1)),
                pl.BlockSpec(
                    (1, tokens, width + LANES),
                    lambda j, c: ((c[1] + 2 * RUN - 2 * c[0] - j) % RUN, 0, 0),
                ),
            ],
            out_specs=[pl.BlockSpec((PAIR, width), lambda j, c: (0, j))] * GROUPS,
        ),
        out_shape=[jax.ShapeDtypeStruct((PAIR, 2 * width), jnp.bfloat16)] * GROUPS,
        compiler_params=params(24),
        name="send_c",
    )(jnp.stack([core, y]), want_to, packed)
    send_c = list(send_c)
    got_h, send_c[0] = lax.optimization_barrier((got_h, send_c[0]))
    got_h = pl.pallas_call(
        order_kernel,
        out_shape=jax.ShapeDtypeStruct((2 * ROWS, hidden), jnp.bfloat16),
        compiler_params=params(16),
        name="order_h",
    )(order, got_h)
    all_h = lax.all_gather(got_h, "ep", axis_index_groups=SAME_RUN, axis=0, tiled=False)

    got_c = [send_c[0]]
    for step, block in zip(SHIFTS[1:], send_c[1:], strict=True):
        got_c.append(lax.ppermute(block, ("ep", "dp"), nearest(*step)))
    got_c = [
        pl.pallas_call(
            join_kernel,
            out_shape=jax.ShapeDtypeStruct((ROWS, 2 * width), jnp.bfloat16),
            compiler_params=params(16),
            name="join",
        )(*part)
        for part in (got_c[:HALF], got_c[HALF:])
    ]
    mate_c = [lax.ppermute(part, "dp", OTHER_CORE) for part in got_c]

    weight = weights[0]
    partial_back = pl.pallas_call(
        back_kernel,
        grid_spec=pltpu.PrefetchScalarGridSpec(
            num_scalar_prefetch=1,
            grid=(RUN,),
            in_specs=[pl.BlockSpec((ROWS, width), lambda s, c: (0, s % 2))] * 4
            + [whole((hidden, width))],
            out_specs=pl.BlockSpec((1, ROWS, hidden), lambda s, c: (s, 0, 0)),
        ),
        out_shape=jax.ShapeDtypeStruct((RUN, ROWS, hidden), jnp.float32),
        compiler_params=params(48),
        name="back",
    )(cores, *got_c, *mate_c, weight)
    summed = lax.psum_scatter(
        partial_back, "ep", scatter_dimension=0, axis_index_groups=SAME_RUN, tiled=False
    )
    back = pl.pallas_call(
        unorder_kernel,
        out_shape=jax.ShapeDtypeStruct((ROWS, hidden), jnp.bfloat16),
        compiler_params=params(16),
        name="unorder",
    )(order_own, summed)
    back = lax.all_to_all(back, "ep", 0, 0, axis_index_groups=SAME_Y, tiled=True)
    hidden_out = pl.pallas_call(
        take_kernel,
        out_shape=jax.ShapeDtypeStruct((count, hidden), jnp.bfloat16),
        compiler_params=params(16),
        name="take",
    )(own_row, own_col, want_own, back)
    hidden_out = hidden_out.reshape(top, tokens, hidden).transpose(1, 0, 2)

    block = 128
    grid = hidden // block
    update = pl.pallas_call(
        update_kernel,
        grid_spec=pltpu.PrefetchScalarGridSpec(
            num_scalar_prefetch=1,
            grid=(grid,),
            in_specs=[pl.BlockSpec((RUN, 2 * ROWS, block), lambda i, c: (0, 0, i))]
            + [whole((ROWS, 2 * width))] * 4
            + [pl.BlockSpec((block, width), lambda i, c: (i, 0))] * 3,
            out_specs=pl.BlockSpec((block, width), lambda i, c: (i, 0)),
        ),
        out_shape=jax.ShapeDtypeStruct((hidden, width), jnp.float32),
        compiler_params=params(56),
        name="update",
    )(cores, all_h, *got_c, *mate_c, weight, first_moment[0], second_moment[0])

    spread = update.astype(jnp.float16).reshape(GROUPS, hidden // GROUPS, width)
    spread = lax.all_to_all(spread, "ep", 0, 0, axis_index_groups=SAME_Y, tiled=True)
    placed = lax.all_to_all(spread[source], "ep", 0, 0, axis_index_groups=SAME_Y, tiled=True)
    placed = placed.reshape(1, hidden, width).astype(jnp.float32) * (1.0 / SCALE)
    return (hidden_out, placed)


def solution(mesh):
    return jax.shard_map(
        local,
        mesh=mesh,
        in_specs=(
            P("ep", None, "dp"),
            P("ep", None),
            P("ep", None),
            P("ep", None),
            P("ep", "dp", None),
            P("ep", "dp", None),
            P("ep", "dp", None),
            P(),
            P(),
            P(),
        ),
        out_specs=(P("ep", None, "dp"), P("ep", "dp", None)),
        check_vma=False,
    )
```

```python
import jax
import jax.numpy as jnp
from jax import lax
from jax.experimental import pallas as pl
from jax.experimental.pallas import tpu as pltpu
from jax.sharding import PartitionSpec as P

beta_one = 0.9
beta_two = 0.95
decay = 0.1
epsilon = 1e-08
bias_one = 1.0 - (0.9**50) ** 2
bias_two = 1.0 - (0.95**50) ** 2

RUN = 4
GROUPS = 16
CAP = 24
ROWS = GROUPS * CAP
SCALE = 2048.0
SAME_Y = [[g * RUN + y for g in range(GROUPS)] for y in range(RUN)]
SAME_RUN = [[g * RUN + y for y in range(RUN)] for g in range(GROUPS)]
OTHER_CORE = [(0, 1), (1, 0), (2, 3), (3, 2)]
GRID = 4
SHIFTS = [(0, 0), (2, 2), (1, 2), (3, 2), (2, 1), (2, 3), (1, 1), (3, 3)]
SHIFTS += [(1, 3), (3, 1), (0, 2), (2, 0), (0, 1), (0, 3), (1, 0), (3, 0)]
HALF = GROUPS // 2
LANES = 128
MB = 1024 * 1024


def contract(a, b, dims):
    return lax.dot_general(a, b, ((dims[0], dims[1]), ((), ())), preferred_element_type=jnp.float32)


def order_of(index, tokens):
    return 2 * (index % tokens) + index // tokens


def choose(row, col, want):
    count = row.shape[1]
    tokens = count // 2
    lane = order_of(lax.broadcasted_iota(jnp.int32, (count, count), 1), tokens)
    line = order_of(lax.broadcasted_iota(jnp.int32, (count, count), 0), tokens)
    ahead = jnp.where((row == col) & (line < lane), 1.0, 0.0)
    position = jnp.sum(ahead, axis=0, keepdims=True)
    place = (lax.broadcasted_iota(jnp.int32, (want.shape[0], 1), 0) % CAP).astype(jnp.float32)
    return (row == want) & (position == place)


def along_y(step):
    return [(i, i // RUN * RUN + (i + step) % RUN) for i in range(GROUPS * RUN)]


def nearest(step_x, step_z):
    pairs = []
    for i in range(GROUPS * RUN):
        x, z_low, y = i // (GRID * RUN), i // RUN % GRID, i % RUN
        for d in range(4):
            z = d // 2 * GRID + z_low
            step = (2 if z % 2 == 0 else -2) if step_z == 2 else (-1 if step_z == 3 else step_z)
            to_z = (z + step) % (2 * GRID)
            to = ((x + step_x) % GRID * GRID + to_z % GRID) * RUN + y
            pairs.append((i * 4 + d, to * 4 + to_z // GRID * 2 + d % 2))
    return pairs


def pack_kernel(y_ref, grad_ref, about_ref, *out_refs):
    width = grad_ref.shape[1] // RUN
    tokens = grad_ref.shape[0]
    about = about_ref[...]
    lane = lax.broadcasted_iota(jnp.int32, (tokens, LANES), 1)
    block = jnp.zeros((tokens, LANES), jnp.float32)
    place = 0
    for k in range(4):
        rest = about[:, k : k + 1]
        for _ in range(1 if k < 2 else 3):
            piece = rest.astype(jnp.bfloat16).astype(jnp.float32)
            block = jnp.where(lane == place, piece, block)
            rest = rest - piece
            place += 1
    for step, out_ref in enumerate(out_refs):
        quarter = (y_ref[0] + step) % RUN
        start = pl.multiple_of(quarter * width, LANES)
        out_ref[:, :width] = grad_ref[:, pl.ds(start, width)]
        out_ref[:, width:] = block.astype(jnp.bfloat16)


def send_h_kernel(row_ref, col_ref, want_ref, acts_ref, own_ref, extra_ref):
    for kind, out_ref in enumerate((own_ref, extra_ref)):
        sel = choose(row_ref[0], col_ref[0], want_ref[kind])
        rows = contract(jnp.where(sel, 1.0, 0.0).astype(jnp.bfloat16), acts_ref[...], ((1,), (0,)))
        out_ref[...] = rows.astype(jnp.bfloat16)


def send_c_kernel(core_ref, want_ref, packed_ref, *out_refs):
    tokens = packed_ref.shape[1]
    width = packed_ref.shape[2] - LANES
    block = packed_ref[0, :, width:]
    eye = lax.broadcasted_iota(jnp.int32, (tokens, tokens), 0) == lax.broadcasted_iota(
        jnp.int32, (tokens, tokens), 1
    )
    lines = contract(block, jnp.where(eye, 1.0, 0.0).astype(jnp.bfloat16), ((0,), (0,)))
    columns = block.astype(jnp.float32)
    row = jnp.concatenate([lines[0:1], lines[1:2]], axis=1)
    col = jnp.concatenate([columns[:, 0:1], columns[:, 1:2]], axis=0)
    gates = [lines[2 + 3 * k : 3 + 3 * k] + lines[3 + 3 * k : 4 + 3 * k] for k in range(2)]
    gates = [gates[k] + lines[4 + 3 * k : 5 + 3 * k] for k in range(2)]
    sel = choose(row, col, want_ref[0])
    gate = jnp.sum(
        jnp.where(sel, jnp.concatenate(gates, axis=1), 0.0), axis=1, keepdims=True
    )
    sel = jnp.where(sel, 1.0, 0.0)
    sel = (sel[:, :tokens] + sel[:, tokens:]).astype(jnp.bfloat16)
    rows = gate * contract(sel, packed_ref[0, :, :width], ((1,), (0,)))
    for i, out_ref in enumerate(out_refs):
        out_ref[...] = rows[i * CAP : (i + 1) * CAP].astype(jnp.bfloat16)


def order_kernel(order_ref, value_ref, out_ref):
    lane = lax.broadcasted_iota(jnp.int32, (ROWS, ROWS), 1)
    turn = jnp.where(lane == order_ref[...], 1.0, 0.0).astype(jnp.bfloat16)
    out_ref[...] = contract(turn, value_ref[...], ((1,), (0,))).astype(jnp.bfloat16)


def unorder_kernel(order_ref, value_ref, out_ref):
    lane = lax.broadcasted_iota(jnp.int32, (ROWS, ROWS), 1)
    turn = jnp.where(lane == order_ref[...], 1.0, 0.0).astype(jnp.bfloat16)
    out_ref[...] = contract(turn, value_ref[...].astype(jnp.bfloat16), ((0,), (0,))).astype(
        jnp.bfloat16
    )


def join_kernel(*refs):
    for i in range(0, len(refs) - 1, 2):
        pair = [ref[...].astype(jnp.float32) for ref in refs[i : i + 2]]
        rows = jnp.concatenate(pair, axis=0).astype(jnp.bfloat16)
        refs[-1][i * CAP : (i + 2) * CAP] = rows


def back_kernel(core_ref, *refs):
    own_refs, mate_refs = refs[0:2], refs[2:4]
    w_ref, out_ref = refs[4:]
    mine = pl.program_id(0) // 2 == core_ref[0]

    def from_halves(c_refs):
        half = c_refs[0].shape[0]
        for at, c_ref in enumerate(c_refs):
            out_ref[0, at * half : (at + 1) * half] = contract(
                c_ref[...], w_ref[...], ((1,), (1,))
            )

    @pl.when(mine)
    def _():
        from_halves(own_refs)

    @pl.when(jnp.logical_not(mine))
    def _():
        from_halves(mate_refs)


def update_kernel(at_ref, h_own_ref, h_extra_ref, *refs):
    own_refs, mate_refs = refs[0:2], refs[2:4]
    w_ref, m_ref, v_ref, out_ref, rows_ref = refs[4:]
    core, y = at_ref[0], at_ref[1]
    block, width = w_ref.shape
    half = own_refs[0].shape[0]

    @pl.when(pl.program_id(0) == 0)
    def _():
        for c_refs, base in ((own_refs, 2 * core), (mate_refs, 2 - 2 * core)):
            for j in range(2):
                places = (base + j, (y + 2 * RUN - base - j) % RUN)
                for kind, place in enumerate(places):
                    part = 2 * kind + j
                    for at, c_ref in enumerate(c_refs):
                        rows_ref[kind, place, at * half : (at + 1) * half] = c_ref[
                            :, part * width : (part + 1) * width
                        ]

    depth = RUN * ROWS
    total = contract(
        h_own_ref[...].reshape(depth, block), rows_ref[0].reshape(depth, width), ((0,), (0,))
    )
    total += contract(
        h_extra_ref[...].reshape(depth, block), rows_ref[1].reshape(depth, width), ((0,), (0,))
    )
    m_new = beta_one * m_ref[...] + (1.0 - beta_one) * total
    v_new = beta_two * v_ref[...] + (1.0 - beta_two) * total * total
    direction = m_new / bias_one / (jnp.sqrt(v_new / bias_two) + epsilon)
    direction = direction + decay * w_ref[...].astype(jnp.float32)
    out_ref[...] = SCALE * direction


def take_kernel(row_ref, col_ref, want_ref, back_ref, out_ref):
    sel = jnp.where(choose(row_ref[0], col_ref[0], want_ref[0]), 1.0, 0.0).astype(jnp.bfloat16)
    out_ref[...] = contract(sel, back_ref[...], ((0,), (0,))).astype(jnp.bfloat16)


def params(limit):
    return pltpu.CompilerParams(vmem_limit_bytes=limit * MB)


def whole(shape):
    return pl.BlockSpec(shape, lambda *_: (0,) * len(shape))


def local(
    hidden_acts,
    out_grad,
    gate_probs,
    route,
    weights,
    first_moment,
    second_moment,
    old_slot,
    new_slot,
    partner,
):
    tokens, top, hidden = hidden_acts.shape
    count = tokens * top
    width = weights.shape[2]
    index = lax.axis_index("ep").astype(jnp.int32)
    y = index % RUN
    core = (lax.axis_index("dp") % 2).astype(jnp.int32)
    cores = core.reshape(1)

    numbers = jnp.arange(GROUPS, dtype=jnp.int32)
    held = old_slot[None, :] == numbers[:, None]
    own = jnp.sum(jnp.where(held, numbers[None, :], 0), axis=1)
    mate = jnp.sum(jnp.where(held, partner[None, :], 0), axis=1)
    mate = jnp.where(mate == own, -1, mate)
    want = jnp.stack([own, mate]).astype(jnp.float32)
    steps = jnp.array(SHIFTS, jnp.int32)
    x, z = index // (GRID * RUN), index // RUN % GRID
    to = (x + steps[:, 0]) % GRID * GRID + (z + steps[:, 1]) % GRID
    by = (x - steps[:, 0]) % GRID * GRID + (z - steps[:, 1]) % GRID
    want_to = jnp.sum(jnp.where(to[:, None] == numbers[None, :], want[:, None, :], 0.0), axis=2)
    want = jnp.broadcast_to(want[:, :, None], (2, GROUPS, CAP)).reshape(2, ROWS, 1)
    want_to = jnp.broadcast_to(want_to[:, :, None], (2, GROUPS, CAP)).reshape(2, ROWS, 1)
    order = (by[:, None] * CAP + jnp.arange(CAP, dtype=jnp.int32)[None, :]).reshape(ROWS, 1)
    source = jnp.sum(
        jnp.where(new_slot[None, :] == numbers[:, None], old_slot[None, :], 0), axis=1
    )

    routes = route.astype(jnp.float32)
    packed = pl.pallas_call(
        pack_kernel,
        grid_spec=pltpu.PrefetchScalarGridSpec(
            num_scalar_prefetch=1,
            grid=(1,),
            in_specs=[whole((tokens, RUN * width)), whole((tokens, 2 * top))],
            out_specs=[whole((tokens, width + LANES))] * RUN,
        ),
        out_shape=[jax.ShapeDtypeStruct((tokens, width + LANES), jnp.bfloat16)] * RUN,
        compiler_params=params(16),
        name="pack",
    )(y.reshape(1), out_grad, jnp.concatenate([routes, gate_probs], axis=1))
    packed = [packed[0]] + [lax.ppermute(packed[s], "ep", along_y(s)) for s in range(1, RUN)]
    packed = jnp.stack(packed)

    own_row = routes.T.reshape(1, 1, count)
    own_col = own_row.reshape(1, count, 1)
    acts = hidden_acts.transpose(1, 0, 2).reshape(count, hidden)
    sent_h = pl.pallas_call(
        send_h_kernel,
        out_shape=[jax.ShapeDtypeStruct((ROWS, hidden), jnp.bfloat16)] * 2,
        compiler_params=params(16),
        name="send_h",
    )(own_row, own_col, want, acts)
    got_h = [
        lax.all_to_all(part, "ep", 0, 0, axis_index_groups=SAME_Y, tiled=True) for part in sent_h
    ]

    send_c = pl.pallas_call(
        send_c_kernel,
        grid_spec=pltpu.PrefetchScalarGridSpec(
            num_scalar_prefetch=1,
            grid=(2, 2),
            in_specs=[
                pl.BlockSpec((1, ROWS, 1), lambda k, j, c: (k, 0, 0)),
                pl.BlockSpec(
                    (1, tokens, width + LANES),
                    lambda k, j, c: ((c[1] + 2 * RUN - 2 * c[0] - j) % RUN, 0, 0),
                ),
            ],
            out_specs=[pl.BlockSpec((CAP, width), lambda k, j, c: (0, 2 * k + j))] * GROUPS,
        ),
        out_shape=[jax.ShapeDtypeStruct((CAP, 4 * width), jnp.bfloat16)] * GROUPS,
        compiler_params=params(24),
        name="send_c",
    )(jnp.stack([core, y]), want_to, packed)
    send_c = list(send_c)
    got_h[0], send_c[0] = lax.optimization_barrier((got_h[0], send_c[0]))
    got_h = [
        pl.pallas_call(
            order_kernel,
            out_shape=jax.ShapeDtypeStruct((ROWS, hidden), jnp.bfloat16),
            compiler_params=params(16),
            name="order_h",
        )(order, part)
        for part in got_h
    ]
    own_h = lax.all_gather(got_h[0], "ep", axis_index_groups=SAME_RUN, axis=0, tiled=False)
    extra_h = [got_h[1]] + [lax.ppermute(got_h[1], "ep", along_y(s)) for s in range(1, RUN)]
    extra_h = jnp.stack(extra_h)

    got_c = [send_c[0]]
    for step, block in zip(SHIFTS[1:], send_c[1:], strict=True):
        got_c.append(lax.ppermute(block, ("ep", "dp"), nearest(*step)))
    half = ROWS // 2
    got_c = [
        pl.pallas_call(
            join_kernel,
            out_shape=jax.ShapeDtypeStruct((half, 4 * width), jnp.bfloat16),
            compiler_params=params(16),
            name="join",
        )(*part)
        for part in (got_c[:HALF], got_c[HALF:])
    ]
    mate_c = [lax.ppermute(part, "dp", OTHER_CORE) for part in got_c]

    weight = weights[0]
    partial_back = pl.pallas_call(
        back_kernel,
        grid_spec=pltpu.PrefetchScalarGridSpec(
            num_scalar_prefetch=1,
            grid=(RUN,),
            in_specs=[pl.BlockSpec((half, width), lambda s, c: (0, s % 2))] * 4
            + [whole((hidden, width))],
            out_specs=pl.BlockSpec((1, ROWS, hidden), lambda s, c: (s, 0, 0)),
        ),
        out_shape=jax.ShapeDtypeStruct((RUN, ROWS, hidden), jnp.float32),
        compiler_params=params(48),
        name="back",
    )(cores, *got_c, *mate_c, weight)
    summed = lax.psum_scatter(
        partial_back, "ep", scatter_dimension=0, axis_index_groups=SAME_RUN, tiled=False
    )
    back = pl.pallas_call(
        unorder_kernel,
        out_shape=jax.ShapeDtypeStruct((ROWS, hidden), jnp.bfloat16),
        compiler_params=params(16),
        name="unorder",
    )(order, summed)
    back = lax.all_to_all(back, "ep", 0, 0, axis_index_groups=SAME_Y, tiled=True)
    hidden_out = pl.pallas_call(
        take_kernel,
        out_shape=jax.ShapeDtypeStruct((count, hidden), jnp.bfloat16),
        compiler_params=params(16),
        name="take",
    )(own_row, own_col, want, back)
    hidden_out = hidden_out.reshape(top, tokens, hidden).transpose(1, 0, 2)

    block = 128
    grid = hidden // block
    update = pl.pallas_call(
        update_kernel,
        grid_spec=pltpu.PrefetchScalarGridSpec(
            num_scalar_prefetch=1,
            grid=(grid,),
            in_specs=[pl.BlockSpec((RUN, ROWS, block), lambda i, c: (0, 0, i))] * 2
            + [whole((half, 4 * width))] * 4
            + [pl.BlockSpec((block, width), lambda i, c: (i, 0))] * 3,
            out_specs=pl.BlockSpec((block, width), lambda i, c: (i, 0)),
            scratch_shapes=[pltpu.VMEM((2, RUN, ROWS, width), jnp.bfloat16)],
        ),
        out_shape=jax.ShapeDtypeStruct((hidden, width), jnp.float32),
        compiler_params=params(48),
        name="update",
    )(
        jnp.stack([core, y]),
        own_h,
        extra_h,
        *got_c,
        *mate_c,
        weight,
        first_moment[0],
        second_moment[0],
    )

    spread = update.astype(jnp.float16).reshape(GROUPS, hidden // GROUPS, width)
    spread = lax.all_to_all(spread, "ep", 0, 0, axis_index_groups=SAME_Y, tiled=True)
    placed = lax.all_to_all(spread[source], "ep", 0, 0, axis_index_groups=SAME_Y, tiled=True)
    placed = placed.reshape(1, hidden, width).astype(jnp.float32) * (1.0 / SCALE)
    return (hidden_out, placed)


def solution(mesh):
    return jax.shard_map(
        local,
        mesh=mesh,
        in_specs=(
            P("ep", None, "dp"),
            P("ep", None),
            P("ep", None),
            P("ep", None),
            P("ep", "dp", None),
            P("ep", "dp", None),
            P("ep", "dp", None),
            P(),
            P(),
            P(),
        ),
        out_specs=(P("ep", None, "dp"), P("ep", "dp", None)),
        check_vma=False,
    )
```

```python
import jax
import jax.numpy as jnp
from jax import lax
from jax.experimental import pallas as pl
from jax.experimental.pallas import tpu as pltpu
from jax.sharding import PartitionSpec as P

beta_one = 0.9
beta_two = 0.95
decay = 0.1
epsilon = 1e-08
bias_one = 1.0 - (0.9**50) ** 2
bias_two = 1.0 - (0.95**50) ** 2

RUN = 4
GROUPS = 16
CAP = 24
ROWS = GROUPS * CAP
SCALE = 2048.0
BACK_SCALE = 16.0
SAME_Y = [[g * RUN + y for g in range(GROUPS)] for y in range(RUN)]
SAME_RUN = [[g * RUN + y for y in range(RUN)] for g in range(GROUPS)]
OTHER_CORE = [(0, 1), (1, 0), (2, 3), (3, 2)]
GRID = 4
SHIFTS = [
    [(0, 0), (2, 2), (1, 2), (2, 1), (3, 3), (0, 3), (1, 0), (1, 1)],
    [(2, 0), (3, 2), (2, 3), (1, 3), (0, 2), (3, 1), (0, 1), (3, 0)],
]
HALF = GROUPS // 2
LANES = 128
MB = 1024 * 1024


def contract(a, b, dims):
    return lax.dot_general(a, b, ((dims[0], dims[1]), ((), ())), preferred_element_type=jnp.float32)


def order_of(index, tokens):
    return 2 * (index % tokens) + index // tokens


def choose(row, col, want):
    count = row.shape[1]
    tokens = count // 2
    lane = order_of(lax.broadcasted_iota(jnp.int32, (count, count), 1), tokens)
    line = order_of(lax.broadcasted_iota(jnp.int32, (count, count), 0), tokens)
    ahead = jnp.where((row == col) & (line < lane), 1.0, 0.0)
    position = jnp.sum(ahead, axis=0, keepdims=True)
    place = (lax.broadcasted_iota(jnp.int32, (want.shape[0], 1), 0) % CAP).astype(jnp.float32)
    return (row == want) & (position == place)


def along_y(step):
    return [(i, i // RUN * RUN + (i + step) % RUN) for i in range(GROUPS * RUN)]


def nearest(number):
    pairs = []
    for i in range(GROUPS * RUN):
        x, z_low, y = i // (GRID * RUN), i // RUN % GRID, i % RUN
        for d in range(4):
            step_x, step_z = SHIFTS[d % 2][number]
            z = d // 2 * GRID + z_low
            step = (2 if z % 2 == 0 else -2) if step_z == 2 else (-1 if step_z == 3 else step_z)
            to_z = (z + step) % (2 * GRID)
            to = ((x + step_x) % GRID * GRID + to_z % GRID) * RUN + y
            pairs.append((i * 4 + d, to * 4 + to_z // GRID * 2 + d % 2))
    return pairs


def pack_kernel(y_ref, grad_ref, about_ref, *out_refs):
    width = grad_ref.shape[1] // RUN
    tokens = grad_ref.shape[0]
    about = about_ref[...]
    lane = lax.broadcasted_iota(jnp.int32, (tokens, LANES), 1)
    block = jnp.zeros((tokens, LANES), jnp.float32)
    place = 0
    for k in range(4):
        rest = about[:, k : k + 1]
        for _ in range(1 if k < 2 else 3):
            piece = rest.astype(jnp.bfloat16).astype(jnp.float32)
            block = jnp.where(lane == place, piece, block)
            rest = rest - piece
            place += 1
    for step, out_ref in enumerate(out_refs):
        quarter = (y_ref[0] + step) % RUN
        start = pl.multiple_of(quarter * width, LANES)
        out_ref[:, :width] = grad_ref[:, pl.ds(start, width)]
        out_ref[:, width:] = block.astype(jnp.bfloat16)


def send_h_kernel(row_ref, col_ref, want_ref, acts_ref, out_ref):
    sel = jnp.where(choose(row_ref[0], col_ref[0], want_ref[...]), 1.0, 0.0).astype(jnp.bfloat16)
    out_ref[...] = contract(sel, acts_ref[...], ((1,), (0,))).astype(jnp.bfloat16)


def send_c_kernel(y_ref, want_ref, packed_ref, *out_refs):
    tokens = packed_ref.shape[1]
    width = packed_ref.shape[2] - LANES
    block = packed_ref[0, :, width:]
    eye = lax.broadcasted_iota(jnp.int32, (tokens, tokens), 0) == lax.broadcasted_iota(
        jnp.int32, (tokens, tokens), 1
    )
    lines = contract(block, jnp.where(eye, 1.0, 0.0).astype(jnp.bfloat16), ((0,), (0,)))
    columns = block.astype(jnp.float32)
    row = jnp.concatenate([lines[0:1], lines[1:2]], axis=1)
    col = jnp.concatenate([columns[:, 0:1], columns[:, 1:2]], axis=0)
    gates = [lines[2 + 3 * k : 3 + 3 * k] + lines[3 + 3 * k : 4 + 3 * k] for k in range(2)]
    gates = [gates[k] + lines[4 + 3 * k : 5 + 3 * k] for k in range(2)]
    sel = choose(row, col, want_ref[0])
    gate = jnp.sum(
        jnp.where(sel, jnp.concatenate(gates, axis=1), 0.0), axis=1, keepdims=True
    )
    sel = jnp.where(sel, 1.0, 0.0)
    sel = (sel[:, :tokens] + sel[:, tokens:]).astype(jnp.bfloat16)
    rows = gate * contract(sel, packed_ref[0, :, :width], ((1,), (0,)))
    for i, out_ref in enumerate(out_refs):
        out_ref[...] = rows[i * CAP : (i + 1) * CAP].astype(jnp.bfloat16)


def order_kernel(order_ref, value_ref, out_ref):
    width = value_ref.shape[1]
    lane = lax.broadcasted_iota(jnp.int32, (ROWS, 2 * ROWS), 1)
    for kind in range(2):
        turn = jnp.where(lane == order_ref[kind], 1.0, 0.0).astype(jnp.bfloat16)
        rows = contract(turn, value_ref[...], ((1,), (0,))).astype(jnp.bfloat16)
        out_ref[:, kind * width : (kind + 1) * width] = rows


def unorder_kernel(order_ref, value_ref, out_ref):
    lane = lax.broadcasted_iota(jnp.int32, (ROWS, ROWS), 1)
    turn = jnp.where(lane == order_ref[...], 1.0, 0.0).astype(jnp.bfloat16)
    out_ref[...] = contract(turn, value_ref[...].astype(jnp.bfloat16), ((0,), (0,))).astype(
        jnp.bfloat16
    )


def join_kernel(*refs):
    for i in range(0, len(refs) - 1, 2):
        pair = [ref[...].astype(jnp.float32) for ref in refs[i : i + 2]]
        rows = jnp.concatenate(pair, axis=0).astype(jnp.bfloat16)
        refs[-1][i * CAP : (i + 2) * CAP] = rows


def back_kernel(*refs):
    w_ref, out_ref, rows_ref = refs[-3:]
    quarter = refs[0].shape[0]
    for at, ref in enumerate(refs[:-3]):
        rows_ref[at * quarter : (at + 1) * quarter] = ref[...]
    out_ref[0] = contract(rows_ref[...], w_ref[...], ((1,), (1,)))


def update_kernel(h_own_ref, h_extra_ref, *refs):
    c_refs = refs[:4]
    w_ref, m_ref, v_ref, out_ref, rows_ref = refs[4:]
    block, width = w_ref.shape
    quarter = c_refs[0].shape[0]

    @pl.when(pl.program_id(0) == 0)
    def _():
        for part in range(2 * RUN):
            for at, c_ref in enumerate(c_refs):
                rows_ref[part, at * quarter : (at + 1) * quarter] = c_ref[
                    :, part * width : (part + 1) * width
                ]

    depth = RUN * ROWS
    total = contract(
        h_own_ref[...].reshape(depth, block), rows_ref[:RUN].reshape(depth, width), ((0,), (0,))
    )
    total += contract(
        h_extra_ref[...].reshape(depth, block), rows_ref[RUN:].reshape(depth, width), ((0,), (0,))
    )
    m_new = beta_one * m_ref[...] + (1.0 - beta_one) * total
    v_new = beta_two * v_ref[...] + (1.0 - beta_two) * total * total
    direction = m_new / bias_one / (jnp.sqrt(v_new / bias_two) + epsilon)
    direction = direction + decay * w_ref[...].astype(jnp.float32)
    out_ref[...] = SCALE * direction


def take_kernel(row_ref, col_ref, want_ref, back_ref, out_ref):
    sel = jnp.where(choose(row_ref[0], col_ref[0], want_ref[...]), 1.0, 0.0).astype(jnp.bfloat16)
    out_ref[...] = contract(sel, back_ref[...], ((0,), (0,))).astype(jnp.bfloat16)


def in_hbm(value):
    return pltpu.with_memory_space_constraint(value, pltpu.HBM)


def params(limit):
    return pltpu.CompilerParams(vmem_limit_bytes=limit * MB)


def whole(shape):
    return pl.BlockSpec(shape, lambda *_: (0,) * len(shape))


def local(
    hidden_acts,
    out_grad,
    gate_probs,
    route,
    weights,
    first_moment,
    second_moment,
    old_slot,
    new_slot,
    partner,
):
    tokens, top, hidden = hidden_acts.shape
    count = tokens * top
    width = weights.shape[2]
    index = lax.axis_index("ep").astype(jnp.int32)
    y = index % RUN
    core = (lax.axis_index("dp") % 2).astype(jnp.int32)

    numbers = jnp.arange(GROUPS, dtype=jnp.int32)
    held = old_slot[None, :] == numbers[:, None]
    own = jnp.sum(jnp.where(held, numbers[None, :], 0), axis=1)
    mate = jnp.sum(jnp.where(held, partner[None, :], 0), axis=1)
    mate = jnp.where(mate == own, -1, mate)
    want = jnp.stack([own, mate]).astype(jnp.float32)
    steps = jnp.array([SHIFTS[0] + SHIFTS[1], SHIFTS[1] + SHIFTS[0]], jnp.int32)
    steps = jnp.where(core == 0, steps[0], steps[1])
    x, z = index // (GRID * RUN), index // RUN % GRID
    to = (x + steps[:HALF, 0]) % GRID * GRID + (z + steps[:HALF, 1]) % GRID
    by = (x - steps[:, 0]) % GRID * GRID + (z - steps[:, 1]) % GRID
    want_to = jnp.sum(jnp.where(to[:, None] == numbers[None, :], want[:, None, :], 0.0), axis=2)
    want_h = jnp.broadcast_to(want.T[:, :, None], (GROUPS, 2, CAP)).reshape(2 * ROWS, 1)
    want = jnp.broadcast_to(want[0, :, None], (GROUPS, CAP)).reshape(ROWS, 1)
    want_to = jnp.broadcast_to(want_to[:, :, None], (2, HALF, CAP)).reshape(2, ROWS // 2, 1)
    place = jnp.arange(CAP, dtype=jnp.int32)[None, :]
    order = (by[:, None] * CAP + place).reshape(ROWS, 1)
    order_h = jnp.stack([by[:, None] * 2 * CAP + place, by[:, None] * 2 * CAP + CAP + place])
    order_h = order_h.reshape(2, ROWS, 1)
    source = jnp.sum(
        jnp.where(new_slot[None, :] == numbers[:, None], old_slot[None, :], 0), axis=1
    )

    routes = route.astype(jnp.float32)
    packed = pl.pallas_call(
        pack_kernel,
        grid_spec=pltpu.PrefetchScalarGridSpec(
            num_scalar_prefetch=1,
            grid=(1,),
            in_specs=[whole((tokens, RUN * width)), whole((tokens, 2 * top))],
            out_specs=[whole((tokens, width + LANES))] * RUN,
        ),
        out_shape=[jax.ShapeDtypeStruct((tokens, width + LANES), jnp.bfloat16)] * RUN,
        compiler_params=params(16),
        name="pack",
    )(y.reshape(1), out_grad, jnp.concatenate([routes, gate_probs], axis=1))
    packed = [packed[0]] + [lax.ppermute(packed[s], "ep", along_y(s)) for s in range(1, RUN)]
    packed = jnp.stack(packed)

    own_row = routes.T.reshape(1, 1, count)
    own_col = own_row.reshape(1, count, 1)
    acts = hidden_acts.transpose(1, 0, 2).reshape(count, hidden)
    sent_h = pl.pallas_call(
        send_h_kernel,
        out_shape=jax.ShapeDtypeStruct((2 * ROWS, hidden), jnp.bfloat16),
        compiler_params=params(16),
        name="send_h",
    )(own_row, own_col, want_h, acts)
    got_h = lax.all_to_all(sent_h, "ep", 0, 0, axis_index_groups=SAME_Y, tiled=True)

    send_c = pl.pallas_call(
        send_c_kernel,
        grid_spec=pltpu.PrefetchScalarGridSpec(
            num_scalar_prefetch=1,
            grid=(2, RUN),
            in_specs=[
                pl.BlockSpec((1, ROWS // 2, 1), lambda k, s, y: (k, 0, 0)),
                pl.BlockSpec(
                    (1, tokens, width + LANES), lambda k, s, y: ((y[0] + RUN - s) % RUN, 0, 0)
                ),
            ],
            out_specs=[pl.BlockSpec((CAP, width), lambda k, s, y: (0, RUN * k + s))] * HALF,
        ),
        out_shape=[pltpu.HBM((CAP, 2 * RUN * width), jnp.bfloat16)] * HALF,
        compiler_params=params(24),
        name="send_c",
    )(y.reshape(1), want_to, packed)
    send_c = list(send_c)
    got_h, send_c[0] = lax.optimization_barrier((got_h, send_c[0]))
    got_h = pl.pallas_call(
        order_kernel,
        out_shape=jax.ShapeDtypeStruct((ROWS, 2 * hidden), jnp.bfloat16),
        compiler_params=params(16),
        name="order_h",
    )(order_h, got_h)
    all_h = lax.all_gather(got_h, "ep", axis_index_groups=SAME_RUN, axis=0, tiled=False)
    got_c = [lax.ppermute(send_c[i], ("ep", "dp"), nearest(i)) for i in range(HALF)]
    own_c, mate_c = [], []
    for at in range(0, HALF, HALF // 2):
        own_c.append(
            pl.pallas_call(
                join_kernel,
                out_shape=pltpu.HBM((ROWS // 4, 2 * RUN * width), jnp.bfloat16),
                compiler_params=params(16),
                name="join",
            )(*got_c[at : at + HALF // 2])
        )
        mate_c.append(lax.ppermute(own_c[-1], "dp", OTHER_CORE))
    parts = [in_hbm(part) for part in own_c + mate_c]

    weight = weights[0]
    partial_back = pl.pallas_call(
        back_kernel,
        grid=(RUN,),
        in_specs=[pl.BlockSpec((ROWS // 4, width), lambda s: (0, s))] * 4
        + [whole((hidden, width))],
        out_specs=pl.BlockSpec((1, ROWS, hidden), lambda s: (s, 0, 0)),
        scratch_shapes=[pltpu.VMEM((ROWS, width), jnp.bfloat16)],
        out_shape=jax.ShapeDtypeStruct((RUN, ROWS, hidden), jnp.float32),
        compiler_params=params(24),
        name="back",
    )(*parts, in_hbm(weight))
    summed = lax.psum_scatter(
        partial_back, "ep", scatter_dimension=0, axis_index_groups=SAME_RUN, tiled=False
    )
    back = pl.pallas_call(
        unorder_kernel,
        out_shape=jax.ShapeDtypeStruct((ROWS, hidden), jnp.bfloat16),
        compiler_params=params(16),
        name="unorder",
    )(order, summed)
    block = 128
    grid = hidden // block
    update = pl.pallas_call(
        update_kernel,
        grid=(grid,),
        in_specs=[
            pl.BlockSpec((RUN, ROWS, block), lambda i: (0, 0, i)),
            pl.BlockSpec((RUN, ROWS, block), lambda i: (0, 0, grid + i)),
        ]
        + [whole((ROWS // 4, 2 * RUN * width))] * 4
        + [pl.BlockSpec((block, width), lambda i: (i, 0))] * 3,
        out_specs=pl.BlockSpec((block, width), lambda i: (i, 0)),
        scratch_shapes=[pltpu.VMEM((2 * RUN, ROWS, width), jnp.bfloat16)],
        out_shape=jax.ShapeDtypeStruct((hidden, width), jnp.float32),
        compiler_params=params(28),
        name="update",
    )(
        in_hbm(all_h),
        in_hbm(all_h),
        *parts,
        in_hbm(weight),
        in_hbm(first_moment[0]),
        in_hbm(second_moment[0]),
    )

    part = hidden // GROUPS
    spread = update.astype(jnp.float16).reshape(GROUPS, part, width)
    spread = lax.all_to_all(spread, "ep", 0, 0, axis_index_groups=SAME_Y, tiled=True)
    riders = (back.astype(jnp.float32) * BACK_SCALE).astype(jnp.float16)
    riders = riders.reshape(GROUPS, part, CAP * hidden // part)
    placed = jnp.concatenate([spread[source], riders], axis=2)
    placed = lax.all_to_all(placed, "ep", 0, 0, axis_index_groups=SAME_Y, tiled=True)
    back = placed[:, :, width:].astype(jnp.float32) * (1.0 / BACK_SCALE)
    back = back.astype(jnp.bfloat16).reshape(ROWS, hidden)
    hidden_out = pl.pallas_call(
        take_kernel,
        out_shape=jax.ShapeDtypeStruct((count, hidden), jnp.bfloat16),
        compiler_params=params(16),
        name="take",
    )(own_row, own_col, want, back)
    hidden_out = hidden_out.reshape(top, tokens, hidden).transpose(1, 0, 2)
    placed = placed[:, :, :width].astype(jnp.float32).reshape(1, hidden, width) * (1.0 / SCALE)
    return (hidden_out, placed)


def solution(mesh):
    return jax.shard_map(
        local,
        mesh=mesh,
        in_specs=(
            P("ep", None, "dp"),
            P("ep", None),
            P("ep", None),
            P("ep", None),
            P("ep", "dp", None),
            P("ep", "dp", None),
            P("ep", "dp", None),
            P(),
            P(),
            P(),
        ),
        out_specs=(P("ep", None, "dp"), P("ep", "dp", None)),
        check_vma=False,
    )
```

```python
import jax
import jax.numpy as jnp
from jax import lax
from jax.experimental import pallas as pl
from jax.experimental.pallas import tpu as pltpu
from jax.sharding import PartitionSpec as P

beta_one = 0.9
beta_two = 0.95
decay = 0.1
epsilon = 1e-08
bias_one = 1.0 - (0.9**50) ** 2
bias_two = 1.0 - (0.95**50) ** 2

RUN = 4
GROUPS = 16
CAP = 24
ROWS = GROUPS * CAP
SCALE = 2048.0
SAME_Y = [[g * RUN + y for g in range(GROUPS)] for y in range(RUN)]
SAME_RUN = [[g * RUN + y for y in range(RUN)] for g in range(GROUPS)]
OTHER_CORE = [(0, 1), (1, 0), (2, 3), (3, 2)]
GRID = 4
SHIFTS = [
    [(0, 0), (2, 2), (1, 2), (2, 1), (3, 3), (0, 3), (1, 0), (1, 1)],
    [(2, 0), (3, 2), (2, 3), (1, 3), (0, 2), (3, 1), (0, 1), (3, 0)],
]
HALF = GROUPS // 2
LANES = 128
MB = 1024 * 1024


def contract(a, b, dims):
    return lax.dot_general(a, b, ((dims[0], dims[1]), ((), ())), preferred_element_type=jnp.float32)


def order_of(index, tokens):
    return 2 * (index % tokens) + index // tokens


def choose(row, col, want):
    count = row.shape[1]
    tokens = count // 2
    lane = order_of(lax.broadcasted_iota(jnp.int32, (count, count), 1), tokens)
    line = order_of(lax.broadcasted_iota(jnp.int32, (count, count), 0), tokens)
    ahead = jnp.where((row == col) & (line < lane), 1.0, 0.0)
    position = jnp.sum(ahead, axis=0, keepdims=True)
    place = (lax.broadcasted_iota(jnp.int32, (want.shape[0], 1), 0) % CAP).astype(jnp.float32)
    return (row == want) & (position == place)


def along_y(step):
    return [(i, i // RUN * RUN + (i + step) % RUN) for i in range(GROUPS * RUN)]


def along_grid(step_x, step_z):
    pairs = []
    for i in range(GROUPS * RUN):
        x, z, y = i // (GRID * RUN), i // RUN % GRID, i % RUN
        pairs.append((i, ((x + step_x) % GRID * GRID + (z + step_z) % GRID) * RUN + y))
    return pairs


def nearest(number):
    pairs = []
    for i in range(GROUPS * RUN):
        x, z_low, y = i // (GRID * RUN), i // RUN % GRID, i % RUN
        for d in range(4):
            step_x, step_z = SHIFTS[d % 2][number]
            z = d // 2 * GRID + z_low
            step = (2 if z % 2 == 0 else -2) if step_z == 2 else (-1 if step_z == 3 else step_z)
            to_z = (z + step) % (2 * GRID)
            to = ((x + step_x) % GRID * GRID + to_z % GRID) * RUN + y
            pairs.append((i * 4 + d, to * 4 + to_z // GRID * 2 + d % 2))
    return pairs


def pack_kernel(y_ref, grad_ref, about_ref, *out_refs):
    width = grad_ref.shape[1] // RUN
    tokens = grad_ref.shape[0]
    about = about_ref[...]
    lane = lax.broadcasted_iota(jnp.int32, (tokens, LANES), 1)
    block = jnp.zeros((tokens, LANES), jnp.float32)
    place = 0
    for k in range(4):
        rest = about[:, k : k + 1]
        for _ in range(1 if k < 2 else 3):
            piece = rest.astype(jnp.bfloat16).astype(jnp.float32)
            block = jnp.where(lane == place, piece, block)
            rest = rest - piece
            place += 1
    for step, out_ref in enumerate(out_refs):
        quarter = (y_ref[0] + step) % RUN
        start = pl.multiple_of(quarter * width, LANES)
        out_ref[:, :width] = grad_ref[:, pl.ds(start, width)]
        out_ref[:, width:] = block.astype(jnp.bfloat16)


def send_h_kernel(row_ref, col_ref, want_ref, acts_ref, out_ref):
    sel = jnp.where(choose(row_ref[0], col_ref[0], want_ref[...]), 1.0, 0.0).astype(jnp.bfloat16)
    out_ref[...] = contract(sel, acts_ref[...], ((1,), (0,))).astype(jnp.bfloat16)


def send_c_kernel(y_ref, want_ref, packed_ref, *out_refs):
    tokens = packed_ref.shape[1]
    width = packed_ref.shape[2] - LANES
    block = packed_ref[0, :, width:]
    eye = lax.broadcasted_iota(jnp.int32, (tokens, tokens), 0) == lax.broadcasted_iota(
        jnp.int32, (tokens, tokens), 1
    )
    lines = contract(block, jnp.where(eye, 1.0, 0.0).astype(jnp.bfloat16), ((0,), (0,)))
    columns = block.astype(jnp.float32)
    row = jnp.concatenate([lines[0:1], lines[1:2]], axis=1)
    col = jnp.concatenate([columns[:, 0:1], columns[:, 1:2]], axis=0)
    gates = [lines[2 + 3 * k : 3 + 3 * k] + lines[3 + 3 * k : 4 + 3 * k] for k in range(2)]
    gates = [gates[k] + lines[4 + 3 * k : 5 + 3 * k] for k in range(2)]
    sel = choose(row, col, want_ref[0])
    gate = jnp.sum(
        jnp.where(sel, jnp.concatenate(gates, axis=1), 0.0), axis=1, keepdims=True
    )
    sel = jnp.where(sel, 1.0, 0.0)
    sel = (sel[:, :tokens] + sel[:, tokens:]).astype(jnp.bfloat16)
    rows = gate * contract(sel, packed_ref[0, :, :width], ((1,), (0,)))
    for i, out_ref in enumerate(out_refs):
        out_ref[...] = rows[i * CAP : (i + 1) * CAP].astype(jnp.bfloat16)


def order_kernel(order_ref, value_ref, out_ref):
    width = value_ref.shape[1]
    lane = lax.broadcasted_iota(jnp.int32, (ROWS, 2 * ROWS), 1)
    for kind in range(2):
        turn = jnp.where(lane == order_ref[kind], 1.0, 0.0).astype(jnp.bfloat16)
        rows = contract(turn, value_ref[...], ((1,), (0,))).astype(jnp.bfloat16)
        out_ref[:, kind * width : (kind + 1) * width] = rows


def return_kernel(to_ref, from_ref, value_ref, *out_refs):
    turn = jnp.where(to_ref[...] == from_ref[...], 1.0, 0.0).astype(jnp.bfloat16)
    rows = contract(turn, value_ref[...].astype(jnp.bfloat16), ((1,), (0,))).astype(jnp.bfloat16)
    part = ROWS // GRID
    for step, out_ref in enumerate(out_refs):
        out_ref[...] = rows[step * part : (step + 1) * part]


def turn_kernel(*refs):
    values = [ref[...].astype(jnp.float32) for ref in refs[:GRID]]
    for step, out_ref in enumerate(refs[GRID:]):
        rows = [value[step * CAP : (step + 1) * CAP] for value in values]
        out_ref[...] = jnp.concatenate(rows, axis=0).astype(jnp.bfloat16)


def join_kernel(*refs):
    for i in range(0, len(refs) - 1, 2):
        pair = [ref[...].astype(jnp.float32) for ref in refs[i : i + 2]]
        rows = jnp.concatenate(pair, axis=0).astype(jnp.bfloat16)
        refs[-1][i * CAP : (i + 2) * CAP] = rows


def back_kernel(*refs):
    w_ref, out_ref, laid_ref = refs[4], refs[-2], refs[-1]
    quarter = refs[0].shape[0]
    source = pl.program_id(0)
    for kind in range(2):
        for at in range(2):
            rows = refs[2 * kind + at][...]
            laid_ref[kind, source, at * quarter : (at + 1) * quarter] = rows
    out_ref[0] = contract(laid_ref[0, source], w_ref[...], ((1,), (1,)))


def update_kernel(
    h_own_ref, h_extra_ref, own_ref, mate_ref, w_ref, m_ref, v_ref, out_ref
):
    block, width = w_ref.shape
    half = own_ref.shape[2]
    depth = RUN * half
    total = jnp.zeros(w_ref.shape, jnp.float32)
    for kind, h_ref in enumerate((h_own_ref, h_extra_ref)):
        for at, c_ref in enumerate((own_ref, mate_ref)):
            rows = h_ref[:, at * half : (at + 1) * half].reshape(depth, block)
            total += contract(rows, c_ref[kind].reshape(depth, width), ((0,), (0,)))
    m_new = beta_one * m_ref[...] + (1.0 - beta_one) * total
    v_new = beta_two * v_ref[...] + (1.0 - beta_two) * total * total
    direction = m_new / bias_one / (jnp.sqrt(v_new / bias_two) + epsilon)
    direction = direction + decay * w_ref[...].astype(jnp.float32)
    out_ref[...] = SCALE * direction


def take_kernel(row_ref, col_ref, want_ref, *refs):
    sel = jnp.where(choose(row_ref[0], col_ref[0], want_ref[...]), 1.0, 0.0).astype(jnp.bfloat16)
    part = ROWS // GRID
    rows = jnp.zeros(refs[-1].shape, jnp.float32)
    for step, ref in enumerate(refs[:-1]):
        rows += contract(sel[step * part : (step + 1) * part], ref[...], ((0,), (0,)))
    refs[-1][...] = rows.astype(jnp.bfloat16)


def in_hbm(value):
    return pltpu.with_memory_space_constraint(value, pltpu.HBM)


def params(limit):
    return pltpu.CompilerParams(vmem_limit_bytes=limit * MB)


def whole(shape):
    return pl.BlockSpec(shape, lambda *_: (0,) * len(shape))


def local(
    hidden_acts,
    out_grad,
    gate_probs,
    route,
    weights,
    first_moment,
    second_moment,
    old_slot,
    new_slot,
    partner,
):
    tokens, top, hidden = hidden_acts.shape
    count = tokens * top
    width = weights.shape[2]
    index = lax.axis_index("ep").astype(jnp.int32)
    y = index % RUN
    core = (lax.axis_index("dp") % 2).astype(jnp.int32)

    numbers = jnp.arange(GROUPS, dtype=jnp.int32)
    held = old_slot[None, :] == numbers[:, None]
    own = jnp.sum(jnp.where(held, numbers[None, :], 0), axis=1)
    mate = jnp.sum(jnp.where(held, partner[None, :], 0), axis=1)
    mate = jnp.where(mate == own, -1, mate)
    want = jnp.stack([own, mate]).astype(jnp.float32)
    steps = jnp.array([SHIFTS[0] + SHIFTS[1], SHIFTS[1] + SHIFTS[0]], jnp.int32)
    steps = jnp.where(core == 0, steps[0], steps[1])
    x, z = index // (GRID * RUN), index // RUN % GRID
    to = (x + steps[:HALF, 0]) % GRID * GRID + (z + steps[:HALF, 1]) % GRID
    by = (x - steps[:, 0]) % GRID * GRID + (z - steps[:, 1]) % GRID
    want_to = jnp.sum(jnp.where(to[:, None] == numbers[None, :], want[:, None, :], 0.0), axis=2)
    want_h = jnp.broadcast_to(want.T[:, :, None], (GROUPS, 2, CAP)).reshape(2 * ROWS, 1)
    outer, inner = numbers // GRID, numbers % GRID
    home = (x + outer) % GRID * GRID + (z + inner) % GRID
    owner = (x - inner) % GRID * GRID + (z - outer) % GRID
    want = jnp.sum(jnp.where(owner[:, None] == numbers[None, :], want[:1], 0.0), axis=1)
    want = jnp.broadcast_to(want[:, None], (GROUPS, CAP)).reshape(ROWS, 1)
    want_to = jnp.broadcast_to(want_to[:, :, None], (2, HALF, CAP)).reshape(2, ROWS // 2, 1)
    place = jnp.arange(CAP, dtype=jnp.int32)[None, :]
    home_to = (home[:, None] * CAP + place).reshape(ROWS, 1)
    home_from = (by[:, None] * CAP + place).reshape(1, ROWS)
    order_h = jnp.stack([by[:, None] * 2 * CAP + place, by[:, None] * 2 * CAP + CAP + place])
    order_h = order_h.reshape(2, ROWS, 1)
    source = jnp.sum(
        jnp.where(new_slot[None, :] == numbers[:, None], old_slot[None, :], 0), axis=1
    )

    routes = route.astype(jnp.float32)
    packed = pl.pallas_call(
        pack_kernel,
        grid_spec=pltpu.PrefetchScalarGridSpec(
            num_scalar_prefetch=1,
            grid=(1,),
            in_specs=[whole((tokens, RUN * width)), whole((tokens, 2 * top))],
            out_specs=[whole((tokens, width + LANES))] * RUN,
        ),
        out_shape=[jax.ShapeDtypeStruct((tokens, width + LANES), jnp.bfloat16)] * RUN,
        compiler_params=params(8),
        name="pack",
    )(y.reshape(1), out_grad, jnp.concatenate([routes, gate_probs], axis=1))
    packed = [packed[0]] + [lax.ppermute(packed[s], "ep", along_y(s)) for s in range(1, RUN)]
    packed = jnp.stack(packed)

    own_row = routes.T.reshape(1, 1, count)
    own_col = own_row.reshape(1, count, 1)
    acts = hidden_acts.transpose(1, 0, 2).reshape(count, hidden)
    sent_h = pl.pallas_call(
        send_h_kernel,
        out_shape=jax.ShapeDtypeStruct((2 * ROWS, hidden), jnp.bfloat16),
        compiler_params=params(8),
        name="send_h",
    )(own_row, own_col, want_h, acts)
    got_h = lax.all_to_all(sent_h, "ep", 0, 0, axis_index_groups=SAME_Y, tiled=True)

    send_c = pl.pallas_call(
        send_c_kernel,
        grid_spec=pltpu.PrefetchScalarGridSpec(
            num_scalar_prefetch=1,
            grid=(2, RUN),
            in_specs=[
                pl.BlockSpec((1, ROWS // 2, 1), lambda k, s, y: (k, 0, 0)),
                pl.BlockSpec(
                    (1, tokens, width + LANES), lambda k, s, y: ((y[0] + RUN - s) % RUN, 0, 0)
                ),
            ],
            out_specs=[pl.BlockSpec((CAP, width), lambda k, s, y: (0, RUN * k + s))] * HALF,
        ),
        out_shape=[pltpu.HBM((CAP, 2 * RUN * width), jnp.bfloat16)] * HALF,
        compiler_params=params(12),
        name="send_c",
    )(y.reshape(1), want_to, packed)
    send_c = list(send_c)
    got_h, send_c[0] = lax.optimization_barrier((got_h, send_c[0]))
    got_h = pl.pallas_call(
        order_kernel,
        out_shape=jax.ShapeDtypeStruct((ROWS, 2 * hidden), jnp.bfloat16),
        compiler_params=params(8),
        name="order_h",
    )(order_h, got_h)
    all_h = lax.all_gather(got_h, "ep", axis_index_groups=SAME_RUN, axis=0, tiled=False)
    got_c = [lax.ppermute(send_c[i], ("ep", "dp"), nearest(i)) for i in range(HALF)]
    own_c, mate_c = [], []
    for at in range(0, HALF, HALF // 2):
        own_c.append(
            pl.pallas_call(
                join_kernel,
                out_shape=jax.ShapeDtypeStruct((ROWS // 4, 2 * RUN * width), jnp.bfloat16),
                compiler_params=params(8),
                name="join",
            )(*got_c[at : at + HALF // 2])
        )
        mate_c.append(lax.ppermute(own_c[-1], "dp", OTHER_CORE))

    weight = weights[0]
    partial_back, laid = [], []
    for at, pair in enumerate((own_c, mate_c)):
        partial_back, rows = pl.pallas_call(
            back_kernel,
            grid=(RUN,),
            in_specs=[pl.BlockSpec((ROWS // 4, width), lambda s: (0, s))] * 2
            + [pl.BlockSpec((ROWS // 4, width), lambda s: (0, RUN + s))] * 2
            + [whole((hidden, width))]
            + [pl.BlockSpec(memory_space=pl.ANY)] * at,
            out_specs=[
                pl.BlockSpec((1, ROWS // 2, hidden), lambda s, at=at: (s, at, 0)),
                whole((2, RUN, ROWS // 2, width)) if at else pl.BlockSpec(memory_space=pltpu.VMEM),
            ],
            out_shape=[
                pltpu.HBM((RUN, ROWS, hidden), jnp.float32),
                (pltpu.VMEM, pltpu.HBM)[at]((2, RUN, ROWS // 2, width), jnp.bfloat16),
            ],
            input_output_aliases={5: 0} if at else {},
            compiler_params=params(24),
            name="back",
        )(*pair, *pair, in_hbm(weight), *([partial_back] if at else []))
        laid.append(rows)
    summed = lax.psum_scatter(
        partial_back, "ep", scatter_dimension=0, axis_index_groups=SAME_RUN, tiled=False
    )
    part = jax.ShapeDtypeStruct((ROWS // GRID, hidden), jnp.bfloat16)
    back = pl.pallas_call(
        return_kernel, out_shape=[part] * GRID, compiler_params=params(8), name="return"
    )(home_to, home_from, summed)
    back = [back[0]] + [lax.ppermute(back[k], "ep", along_grid(k, 0)) for k in range(1, GRID)]
    back = pl.pallas_call(
        turn_kernel, out_shape=[part] * GRID, compiler_params=params(8), name="turn"
    )(*back)
    back = [back[0]] + [lax.ppermute(back[k], "ep", along_grid(0, k)) for k in range(1, GRID)]
    hidden_out = pl.pallas_call(
        take_kernel,
        out_shape=jax.ShapeDtypeStruct((count, hidden), jnp.bfloat16),
        compiler_params=params(8),
        name="take",
    )(own_row, own_col, want, *back)
    hidden_out = hidden_out.reshape(top, tokens, hidden).transpose(1, 0, 2)

    block = 128
    grid = hidden // block
    update = pl.pallas_call(
        update_kernel,
        grid=(grid,),
        in_specs=[
            pl.BlockSpec((RUN, ROWS, block), lambda i: (0, 0, i)),
            pl.BlockSpec((RUN, ROWS, block), lambda i: (0, 0, grid + i)),
        ]
        + [pl.BlockSpec(memory_space=pltpu.VMEM), whole((2, RUN, ROWS // 2, width))]
        + [pl.BlockSpec((block, width), lambda i: (i, 0))] * 3,
        out_specs=pl.BlockSpec((block, width), lambda i: (i, 0)),
        out_shape=jax.ShapeDtypeStruct((hidden, width), jnp.float32),
        compiler_params=params(24),
        name="update",
    )(
        in_hbm(all_h),
        in_hbm(all_h),
        laid[0],
        in_hbm(laid[1]),
        in_hbm(weight),
        in_hbm(first_moment[0]),
        in_hbm(second_moment[0]),
    )

    spread = update.astype(jnp.float16).reshape(GROUPS, hidden // GROUPS, width)
    spread = lax.all_to_all(spread, "ep", 0, 0, axis_index_groups=SAME_Y, tiled=True)
    placed = lax.all_to_all(spread[source], "ep", 0, 0, axis_index_groups=SAME_Y, tiled=True)
    placed = placed.reshape(1, hidden, width).astype(jnp.float32) * (1.0 / SCALE)
    return (hidden_out, placed)


def solution(mesh):
    return jax.shard_map(
        local,
        mesh=mesh,
        in_specs=(
            P("ep", None, "dp"),
            P("ep", None),
            P("ep", None),
            P("ep", None),
            P("ep", "dp", None),
            P("ep", "dp", None),
            P("ep", "dp", None),
            P(),
            P(),
            P(),
        ),
        out_specs=(P("ep", None, "dp"), P("ep", "dp", None)),
        check_vma=False,
    )
```

```python
import jax
import jax.numpy as jnp
from jax import lax
from jax.experimental import pallas as pl
from jax.experimental.pallas import tpu as pltpu
from jax.sharding import PartitionSpec as P

beta_one = 0.9
beta_two = 0.95
decay = 0.1
epsilon = 1e-08
bias_one = 1.0 - (0.9**50) ** 2
bias_two = 1.0 - (0.95**50) ** 2

RUN = 4
GROUPS = 16
CAP = 24
ROWS = GROUPS * CAP
SCALE = 2048.0
SAME_Y = [[g * RUN + y for g in range(GROUPS)] for y in range(RUN)]
SAME_RUN = [[g * RUN + y for y in range(RUN)] for g in range(GROUPS)]
OTHER_CORE = [(0, 1), (1, 0), (2, 3), (3, 2)]
GRID = 4
SHIFTS = [
    [(0, 0), (2, 2), (1, 2), (2, 1), (3, 3), (0, 3), (1, 0), (1, 1)],
    [(2, 0), (3, 2), (2, 3), (1, 3), (0, 2), (3, 1), (0, 1), (3, 0)],
]
HALF = GROUPS // 2
LANES = 128
MB = 1024 * 1024


def contract(a, b, dims):
    return lax.dot_general(a, b, ((dims[0], dims[1]), ((), ())), preferred_element_type=jnp.float32)


def order_of(index, tokens):
    return 2 * (index % tokens) + index // tokens


def choose(row, col, want):
    count = row.shape[1]
    tokens = count // 2
    lane = order_of(lax.broadcasted_iota(jnp.int32, (count, count), 1), tokens)
    line = order_of(lax.broadcasted_iota(jnp.int32, (count, count), 0), tokens)
    ahead = jnp.where((row == col) & (line < lane), 1.0, 0.0)
    position = jnp.sum(ahead, axis=0, keepdims=True)
    place = (lax.broadcasted_iota(jnp.int32, (want.shape[0], 1), 0) % CAP).astype(jnp.float32)
    return (row == want) & (position == place)


def along_y(step):
    return [(i, i // RUN * RUN + (i + step) % RUN) for i in range(GROUPS * RUN)]


def along_grid(step_x, step_z):
    pairs = []
    for i in range(GROUPS * RUN):
        x, z, y = i // (GRID * RUN), i // RUN % GRID, i % RUN
        pairs.append((i, ((x + step_x) % GRID * GRID + (z + step_z) % GRID) * RUN + y))
    return pairs


def nearest(number):
    pairs = []
    for i in range(GROUPS * RUN):
        x, z_low, y = i // (GRID * RUN), i // RUN % GRID, i % RUN
        for d in range(4):
            step_x, step_z = SHIFTS[d % 2][number]
            z = d // 2 * GRID + z_low
            step = (2 if z % 2 == 0 else -2) if step_z == 2 else (-1 if step_z == 3 else step_z)
            to_z = (z + step) % (2 * GRID)
            to = ((x + step_x) % GRID * GRID + to_z % GRID) * RUN + y
            pairs.append((i * 4 + d, to * 4 + to_z // GRID * 2 + d % 2))
    return pairs


def pack_kernel(y_ref, grad_ref, about_ref, *out_refs):
    width = grad_ref.shape[1] // RUN
    tokens = grad_ref.shape[0]
    about = about_ref[...]
    lane = lax.broadcasted_iota(jnp.int32, (tokens, LANES), 1)
    block = jnp.zeros((tokens, LANES), jnp.float32)
    place = 0
    for k in range(4):
        rest = about[:, k : k + 1]
        for _ in range(1 if k < 2 else 3):
            piece = rest.astype(jnp.bfloat16).astype(jnp.float32)
            block = jnp.where(lane == place, piece, block)
            rest = rest - piece
            place += 1
    for step, out_ref in enumerate(out_refs):
        quarter = (y_ref[0] + step) % RUN
        start = pl.multiple_of(quarter * width, LANES)
        out_ref[:, :width] = grad_ref[:, pl.ds(start, width)]
        out_ref[:, width:] = block.astype(jnp.bfloat16)


def send_h_kernel(row_ref, col_ref, want_ref, acts_ref, out_ref):
    width = acts_ref.shape[1]
    for kind in range(2):
        sel = choose(row_ref[0], col_ref[0], want_ref[kind])
        rows = contract(jnp.where(sel, 1.0, 0.0).astype(jnp.bfloat16), acts_ref[...], ((1,), (0,)))
        out_ref[:, kind * width : (kind + 1) * width] = rows.astype(jnp.bfloat16)


def send_c_kernel(y_ref, want_ref, packed_ref, *out_refs):
    tokens = packed_ref.shape[1]
    width = packed_ref.shape[2] - LANES
    block = packed_ref[0, :, width:]
    eye = lax.broadcasted_iota(jnp.int32, (tokens, tokens), 0) == lax.broadcasted_iota(
        jnp.int32, (tokens, tokens), 1
    )
    lines = contract(block, jnp.where(eye, 1.0, 0.0).astype(jnp.bfloat16), ((0,), (0,)))
    columns = block.astype(jnp.float32)
    row = jnp.concatenate([lines[0:1], lines[1:2]], axis=1)
    col = jnp.concatenate([columns[:, 0:1], columns[:, 1:2]], axis=0)
    gates = [lines[2 + 3 * k : 3 + 3 * k] + lines[3 + 3 * k : 4 + 3 * k] for k in range(2)]
    gates = [gates[k] + lines[4 + 3 * k : 5 + 3 * k] for k in range(2)]
    sel = choose(row, col, want_ref[0])
    gate = jnp.sum(
        jnp.where(sel, jnp.concatenate(gates, axis=1), 0.0), axis=1, keepdims=True
    )
    sel = jnp.where(sel, 1.0, 0.0)
    sel = (sel[:, :tokens] + sel[:, tokens:]).astype(jnp.bfloat16)
    rows = gate * contract(sel, packed_ref[0, :, :width], ((1,), (0,)))
    for i, out_ref in enumerate(out_refs):
        out_ref[...] = rows[i * CAP : (i + 1) * CAP].astype(jnp.bfloat16)


def order_kernel(order_ref, value_ref, out_ref):
    lane = lax.broadcasted_iota(jnp.int32, (ROWS, ROWS), 1)
    turn = jnp.where(lane == order_ref[...], 1.0, 0.0).astype(jnp.bfloat16)
    out_ref[...] = contract(turn, value_ref[...], ((1,), (0,))).astype(jnp.bfloat16)


def return_kernel(to_ref, from_ref, value_ref, *out_refs):
    turn = jnp.where(to_ref[...] == from_ref[...], 1.0, 0.0).astype(jnp.bfloat16)
    rows = contract(turn, value_ref[...].astype(jnp.bfloat16), ((1,), (0,))).astype(jnp.bfloat16)
    part = ROWS // GRID
    for step, out_ref in enumerate(out_refs):
        out_ref[...] = rows[step * part : (step + 1) * part]


def turn_kernel(*refs):
    values = [ref[...].astype(jnp.float32) for ref in refs[:GRID]]
    for step, out_ref in enumerate(refs[GRID:]):
        rows = [value[step * CAP : (step + 1) * CAP] for value in values]
        out_ref[...] = jnp.concatenate(rows, axis=0).astype(jnp.bfloat16)


def join_kernel(*refs):
    for i in range(0, len(refs) - 1, 2):
        pair = [ref[...].astype(jnp.float32) for ref in refs[i : i + 2]]
        rows = jnp.concatenate(pair, axis=0).astype(jnp.bfloat16)
        refs[-1][i * CAP : (i + 2) * CAP] = rows


def back_kernel(*refs):
    w_ref, out_ref, laid_ref = refs[4], refs[-2], refs[-1]
    quarter = refs[0].shape[0]
    source = pl.program_id(0) if laid_ref.shape[1] == RUN else 0
    for kind in range(2):
        for at in range(2):
            rows = refs[2 * kind + at][...]
            laid_ref[kind, source, at * quarter : (at + 1) * quarter] = rows
    out_ref[0] = contract(laid_ref[0, source], w_ref[...], ((1,), (1,)))


def update_kernel(
    h_own_ref, h_extra_ref, own_ref, first_ref, second_ref, w_ref, m_ref, v_ref, out_ref
):
    block, width = w_ref.shape
    half = own_ref.shape[2]
    depth = RUN * half
    total = jnp.zeros(w_ref.shape, jnp.float32)
    for kind, h_ref in enumerate((h_own_ref, h_extra_ref)):
        for at, part in enumerate((own_ref[kind], (first_ref, second_ref)[kind][0])):
            rows = h_ref[:, at * half : (at + 1) * half].reshape(depth, block)
            total += contract(rows, part.reshape(depth, width), ((0,), (0,)))
    m_new = beta_one * m_ref[...] + (1.0 - beta_one) * total
    v_new = beta_two * v_ref[...] + (1.0 - beta_two) * total * total
    direction = m_new / bias_one / (jnp.sqrt(v_new / bias_two) + epsilon)
    direction = direction + decay * w_ref[...].astype(jnp.float32)
    out_ref[...] = SCALE * direction


def take_kernel(row_ref, col_ref, want_ref, *refs):
    sel = jnp.where(choose(row_ref[0], col_ref[0], want_ref[...]), 1.0, 0.0).astype(jnp.bfloat16)
    part = ROWS // GRID
    rows = jnp.zeros(refs[-1].shape, jnp.float32)
    for step, ref in enumerate(refs[:-1]):
        rows += contract(sel[step * part : (step + 1) * part], ref[...], ((0,), (0,)))
    refs[-1][...] = rows.astype(jnp.bfloat16)


def in_hbm(value):
    return pltpu.with_memory_space_constraint(value, pltpu.HBM)


def params(limit):
    return pltpu.CompilerParams(vmem_limit_bytes=limit * MB)


def whole(shape):
    return pl.BlockSpec(shape, lambda *_: (0,) * len(shape))


def local(
    hidden_acts,
    out_grad,
    gate_probs,
    route,
    weights,
    first_moment,
    second_moment,
    old_slot,
    new_slot,
    partner,
):
    tokens, top, hidden = hidden_acts.shape
    count = tokens * top
    width = weights.shape[2]
    index = lax.axis_index("ep").astype(jnp.int32)
    y = index % RUN
    core = (lax.axis_index("dp") % 2).astype(jnp.int32)

    numbers = jnp.arange(GROUPS, dtype=jnp.int32)
    held = old_slot[None, :] == numbers[:, None]
    own = jnp.sum(jnp.where(held, numbers[None, :], 0), axis=1)
    mate = jnp.sum(jnp.where(held, partner[None, :], 0), axis=1)
    mate = jnp.where(mate == own, -1, mate)
    want = jnp.stack([own, mate]).astype(jnp.float32)
    steps = jnp.array([SHIFTS[0] + SHIFTS[1], SHIFTS[1] + SHIFTS[0]], jnp.int32)
    steps = jnp.where(core == 0, steps[0], steps[1])
    x, z = index // (GRID * RUN), index // RUN % GRID
    to = (x + steps[:HALF, 0]) % GRID * GRID + (z + steps[:HALF, 1]) % GRID
    by = (x - steps[:, 0]) % GRID * GRID + (z - steps[:, 1]) % GRID
    want_to = jnp.sum(jnp.where(to[:, None] == numbers[None, :], want[:, None, :], 0.0), axis=2)
    want_h = jnp.broadcast_to(want[:, :, None], (2, GROUPS, CAP)).reshape(2, ROWS, 1)
    outer, inner = numbers // GRID, numbers % GRID
    home = (x + outer) % GRID * GRID + (z + inner) % GRID
    owner = (x - inner) % GRID * GRID + (z - outer) % GRID
    want = jnp.sum(jnp.where(owner[:, None] == numbers[None, :], want[:1], 0.0), axis=1)
    want = jnp.broadcast_to(want[:, None], (GROUPS, CAP)).reshape(ROWS, 1)
    want_to = jnp.broadcast_to(want_to[:, :, None], (2, HALF, CAP)).reshape(2, ROWS // 2, 1)
    place = jnp.arange(CAP, dtype=jnp.int32)[None, :]
    home_to = (home[:, None] * CAP + place).reshape(ROWS, 1)
    home_from = (by[:, None] * CAP + place).reshape(1, ROWS)
    order_h = (by[:, None] * CAP + place).reshape(ROWS, 1)
    source = jnp.sum(
        jnp.where(new_slot[None, :] == numbers[:, None], old_slot[None, :], 0), axis=1
    )

    routes = route.astype(jnp.float32)
    packed = pl.pallas_call(
        pack_kernel,
        grid_spec=pltpu.PrefetchScalarGridSpec(
            num_scalar_prefetch=1,
            grid=(1,),
            in_specs=[whole((tokens, RUN * width)), whole((tokens, 2 * top))],
            out_specs=[whole((tokens, width + LANES))] * RUN,
        ),
        out_shape=[jax.ShapeDtypeStruct((tokens, width + LANES), jnp.bfloat16)] * RUN,
        compiler_params=params(8),
        name="pack",
    )(y.reshape(1), out_grad, jnp.concatenate([routes, gate_probs], axis=1))
    packed = [packed[0]] + [lax.ppermute(packed[s], "ep", along_y(s)) for s in range(1, RUN)]
    packed = jnp.stack(packed)

    own_row = routes.T.reshape(1, 1, count)
    own_col = own_row.reshape(1, count, 1)
    acts = hidden_acts.transpose(1, 0, 2).reshape(count, hidden)
    sent_h = pl.pallas_call(
        send_h_kernel,
        out_shape=jax.ShapeDtypeStruct((ROWS, 2 * hidden), jnp.bfloat16),
        compiler_params=params(8),
        name="send_h",
    )(own_row, own_col, want_h, acts)
    got_h = lax.all_to_all(sent_h, "ep", 0, 0, axis_index_groups=SAME_Y, tiled=True)

    send_c = pl.pallas_call(
        send_c_kernel,
        grid_spec=pltpu.PrefetchScalarGridSpec(
            num_scalar_prefetch=1,
            grid=(2, RUN),
            in_specs=[
                pl.BlockSpec((1, ROWS // 2, 1), lambda k, s, y: (k, 0, 0)),
                pl.BlockSpec(
                    (1, tokens, width + LANES), lambda k, s, y: ((y[0] + RUN - s) % RUN, 0, 0)
                ),
            ],
            out_specs=[pl.BlockSpec((CAP, width), lambda k, s, y: (0, RUN * k + s))] * HALF,
        ),
        out_shape=[pltpu.HBM((CAP, 2 * RUN * width), jnp.bfloat16)] * HALF,
        compiler_params=params(12),
        name="send_c",
    )(y.reshape(1), want_to, packed)
    send_c = list(send_c)
    got_h, send_c[0] = lax.optimization_barrier((got_h, send_c[0]))
    got_h = pl.pallas_call(
        order_kernel,
        out_shape=jax.ShapeDtypeStruct((ROWS, 2 * hidden), jnp.bfloat16),
        compiler_params=params(8),
        name="order_h",
    )(order_h, got_h)
    all_h = lax.all_gather(got_h, "ep", axis_index_groups=SAME_RUN, axis=0, tiled=False)
    got_c = [lax.ppermute(send_c[i], ("ep", "dp"), nearest(i)) for i in range(HALF)]
    own_c, mate_c = [], []
    for at in range(0, HALF, HALF // 2):
        own_c.append(
            pl.pallas_call(
                join_kernel,
                out_shape=jax.ShapeDtypeStruct((ROWS // 4, 2 * RUN * width), jnp.bfloat16),
                compiler_params=params(8),
                name="join",
            )(*got_c[at : at + HALF // 2])
        )
        mate_c.append(lax.ppermute(own_c[-1], "dp", OTHER_CORE))

    weight = weights[0]
    partial_back, laid = [], []
    for at, pair in enumerate((own_c, mate_c)):
        partial_back, rows = pl.pallas_call(
            back_kernel,
            grid=(RUN,),
            in_specs=[pl.BlockSpec((ROWS // 4, width), lambda s: (0, s))] * 2
            + [pl.BlockSpec((ROWS // 4, width), lambda s: (0, RUN + s))] * 2
            + [whole((hidden, width))]
            + [pl.BlockSpec(memory_space=pl.ANY)] * at,
            out_specs=[
                pl.BlockSpec((1, ROWS // 2, hidden), lambda s, at=at: (s, at, 0)),
                pl.BlockSpec((2, 1, ROWS // 2, width), lambda s: (0, s, 0, 0))
                if at
                else pl.BlockSpec(memory_space=pltpu.VMEM),
            ],
            out_shape=[
                pltpu.HBM((RUN, ROWS, hidden), jnp.float32),
                (pltpu.VMEM, pltpu.HBM)[at]((2, RUN, ROWS // 2, width), jnp.bfloat16),
            ],
            input_output_aliases={5: 0} if at else {},
            compiler_params=params(24),
            name="back",
        )(*pair, *pair, in_hbm(weight), *([partial_back] if at else []))
        laid.append(rows)
    summed = lax.psum_scatter(
        partial_back, "ep", scatter_dimension=0, axis_index_groups=SAME_RUN, tiled=False
    )
    part = jax.ShapeDtypeStruct((ROWS // GRID, hidden), jnp.bfloat16)
    back = pl.pallas_call(
        return_kernel, out_shape=[part] * GRID, compiler_params=params(8), name="return"
    )(home_to, home_from, summed)
    back = [back[0]] + [lax.ppermute(back[k], "ep", along_grid(k, 0)) for k in range(1, GRID)]
    back = pl.pallas_call(
        turn_kernel, out_shape=[part] * GRID, compiler_params=params(8), name="turn"
    )(*back)
    back = [back[0]] + [lax.ppermute(back[k], "ep", along_grid(0, k)) for k in range(1, GRID)]
    hidden_out = pl.pallas_call(
        take_kernel,
        out_shape=jax.ShapeDtypeStruct((count, hidden), jnp.bfloat16),
        compiler_params=params(8),
        name="take",
    )(own_row, own_col, want, *back)
    hidden_out = hidden_out.reshape(top, tokens, hidden).transpose(1, 0, 2)

    block = 128
    grid = hidden // block
    update = pl.pallas_call(
        update_kernel,
        grid=(grid,),
        in_specs=[
            pl.BlockSpec((RUN, ROWS, block), lambda i: (0, 0, i)),
            pl.BlockSpec((RUN, ROWS, block), lambda i: (0, 0, grid + i)),
        ]
        + [pl.BlockSpec(memory_space=pltpu.VMEM)]
        + [
            pl.BlockSpec((1, RUN, ROWS // 2, width), lambda i, k=k: (k, 0, 0, 0))
            for k in range(2)
        ]
        + [pl.BlockSpec((block, width), lambda i: (i, 0))] * 3,
        out_specs=pl.BlockSpec((block, width), lambda i: (i, 0)),
        out_shape=jax.ShapeDtypeStruct((hidden, width), jnp.float32),
        compiler_params=params(24),
        name="update",
    )(
        in_hbm(all_h),
        in_hbm(all_h),
        laid[0],
        in_hbm(laid[1]),
        in_hbm(laid[1]),
        in_hbm(weight),
        in_hbm(first_moment[0]),
        in_hbm(second_moment[0]),
    )

    spread = update.astype(jnp.float16).reshape(GROUPS, hidden // GROUPS, width)
    spread = lax.all_to_all(spread, "ep", 0, 0, axis_index_groups=SAME_Y, tiled=True)
    placed = lax.all_to_all(spread[source], "ep", 0, 0, axis_index_groups=SAME_Y, tiled=True)
    placed = placed.reshape(1, hidden, width).astype(jnp.float32) * (1.0 / SCALE)
    return (hidden_out, placed)


def solution(mesh):
    return jax.shard_map(
        local,
        mesh=mesh,
        in_specs=(
            P("ep", None, "dp"),
            P("ep", None),
            P("ep", None),
            P("ep", None),
            P("ep", "dp", None),
            P("ep", "dp", None),
            P("ep", "dp", None),
            P(),
            P(),
            P(),
        ),
        out_specs=(P("ep", None, "dp"), P("ep", "dp", None)),
        check_vma=False,
    )
```

```python
import jax
import jax.numpy as jnp
from jax import lax
from jax.experimental import pallas as pl
from jax.experimental.pallas import tpu as pltpu
from jax.sharding import PartitionSpec as P

beta_one = 0.9
beta_two = 0.95
decay = 0.1
epsilon = 1e-08
bias_one = 1.0 - (0.9**50) ** 2
bias_two = 1.0 - (0.95**50) ** 2

RUN = 4
GROUPS = 16
CAP = 24
ROWS = GROUPS * CAP
SCALE = 2048.0
SAME_Y = [[g * RUN + y for g in range(GROUPS)] for y in range(RUN)]
SAME_RUN = [[g * RUN + y for y in range(RUN)] for g in range(GROUPS)]
OTHER_CORE = [(0, 1), (1, 0), (2, 3), (3, 2)]
GRID = 4
SHIFTS = [
    [(0, 0), (2, 2), (1, 2), (2, 1), (3, 3), (0, 3), (1, 0), (1, 1)],
    [(2, 0), (3, 2), (2, 3), (1, 3), (0, 2), (3, 1), (0, 1), (3, 0)],
]
HALF = GROUPS // 2
LANES = 128
MB = 1024 * 1024


def contract(a, b, dims):
    return lax.dot_general(a, b, ((dims[0], dims[1]), ((), ())), preferred_element_type=jnp.float32)


def order_of(index, tokens):
    return 2 * (index % tokens) + index // tokens


def choose(row, col, want):
    count = row.shape[1]
    tokens = count // 2
    lane = order_of(lax.broadcasted_iota(jnp.int32, (count, count), 1), tokens)
    line = order_of(lax.broadcasted_iota(jnp.int32, (count, count), 0), tokens)
    ahead = jnp.where((row == col) & (line < lane), 1.0, 0.0)
    position = jnp.sum(ahead, axis=0, keepdims=True)
    place = (lax.broadcasted_iota(jnp.int32, (want.shape[0], 1), 0) % CAP).astype(jnp.float32)
    return (row == want) & (position == place)


def along_y(step):
    return [(i, i // RUN * RUN + (i + step) % RUN) for i in range(GROUPS * RUN)]


def along_grid(step_x, step_z):
    pairs = []
    for i in range(GROUPS * RUN):
        x, z, y = i // (GRID * RUN), i // RUN % GRID, i % RUN
        pairs.append((i, ((x + step_x) % GRID * GRID + (z + step_z) % GRID) * RUN + y))
    return pairs


def nearest(number):
    pairs = []
    for i in range(GROUPS * RUN):
        x, z_low, y = i // (GRID * RUN), i // RUN % GRID, i % RUN
        for d in range(4):
            step_x, step_z = SHIFTS[d % 2][number]
            z = d // 2 * GRID + z_low
            step = (2 if z % 2 == 0 else -2) if step_z == 2 else (-1 if step_z == 3 else step_z)
            to_z = (z + step) % (2 * GRID)
            to = ((x + step_x) % GRID * GRID + to_z % GRID) * RUN + y
            pairs.append((i * 4 + d, to * 4 + to_z // GRID * 2 + d % 2))
    return pairs


def pack_kernel(y_ref, grad_ref, about_ref, *out_refs):
    width = grad_ref.shape[1] // RUN
    tokens = grad_ref.shape[0]
    about = about_ref[...]
    lane = lax.broadcasted_iota(jnp.int32, (tokens, LANES), 1)
    block = jnp.zeros((tokens, LANES), jnp.float32)
    place = 0
    for k in range(4):
        rest = about[:, k : k + 1]
        for _ in range(1 if k < 2 else 3):
            piece = rest.astype(jnp.bfloat16).astype(jnp.float32)
            block = jnp.where(lane == place, piece, block)
            rest = rest - piece
            place += 1
    for step, out_ref in enumerate(out_refs):
        quarter = (y_ref[0] + step) % RUN
        start = pl.multiple_of(quarter * width, LANES)
        out_ref[:, :width] = grad_ref[:, pl.ds(start, width)]
        out_ref[:, width:] = block.astype(jnp.bfloat16)


def send_h_kernel(row_ref, col_ref, want_ref, acts_ref, out_ref):
    width = acts_ref.shape[1]
    for kind in range(2):
        sel = choose(row_ref[0], col_ref[0], want_ref[kind])
        rows = contract(jnp.where(sel, 1.0, 0.0).astype(jnp.bfloat16), acts_ref[...], ((1,), (0,)))
        out_ref[:, kind * width : (kind + 1) * width] = rows.astype(jnp.bfloat16)


def send_c_kernel(y_ref, want_ref, packed_ref, *out_refs):
    tokens = packed_ref.shape[1]
    width = packed_ref.shape[2] - LANES
    block = packed_ref[0, :, width:]
    eye = lax.broadcasted_iota(jnp.int32, (tokens, tokens), 0) == lax.broadcasted_iota(
        jnp.int32, (tokens, tokens), 1
    )
    lines = contract(block, jnp.where(eye, 1.0, 0.0).astype(jnp.bfloat16), ((0,), (0,)))
    columns = block.astype(jnp.float32)
    row = jnp.concatenate([lines[0:1], lines[1:2]], axis=1)
    col = jnp.concatenate([columns[:, 0:1], columns[:, 1:2]], axis=0)
    gates = [lines[2 + 3 * k : 3 + 3 * k] + lines[3 + 3 * k : 4 + 3 * k] for k in range(2)]
    gates = [gates[k] + lines[4 + 3 * k : 5 + 3 * k] for k in range(2)]
    sel = choose(row, col, want_ref[0])
    gate = jnp.sum(
        jnp.where(sel, jnp.concatenate(gates, axis=1), 0.0), axis=1, keepdims=True
    )
    sel = jnp.where(sel, 1.0, 0.0)
    sel = (sel[:, :tokens] + sel[:, tokens:]).astype(jnp.bfloat16)
    rows = gate * contract(sel, packed_ref[0, :, :width], ((1,), (0,)))
    for i, out_ref in enumerate(out_refs):
        out_ref[...] = rows[i * CAP : (i + 1) * CAP].astype(jnp.bfloat16)


def order_kernel(order_ref, value_ref, out_ref):
    lane = lax.broadcasted_iota(jnp.int32, (ROWS, ROWS), 1)
    turn = jnp.where(lane == order_ref[...], 1.0, 0.0).astype(jnp.bfloat16)
    out_ref[...] = contract(turn, value_ref[...], ((1,), (0,))).astype(jnp.bfloat16)


def return_kernel(to_ref, from_ref, value_ref, *out_refs):
    turn = jnp.where(to_ref[...] == from_ref[...], 1.0, 0.0).astype(jnp.bfloat16)
    rows = contract(turn, value_ref[...].astype(jnp.bfloat16), ((1,), (0,))).astype(jnp.bfloat16)
    part = ROWS // GRID
    for step, out_ref in enumerate(out_refs):
        out_ref[...] = rows[step * part : (step + 1) * part]


def turn_kernel(*refs):
    values = [ref[...].astype(jnp.float32) for ref in refs[:GRID]]
    for step, out_ref in enumerate(refs[GRID:]):
        rows = [value[step * CAP : (step + 1) * CAP] for value in values]
        out_ref[...] = jnp.concatenate(rows, axis=0).astype(jnp.bfloat16)


def join_kernel(*refs):
    for i in range(0, len(refs) - 1, 2):
        pair = [ref[...].astype(jnp.float32) for ref in refs[i : i + 2]]
        rows = jnp.concatenate(pair, axis=0).astype(jnp.bfloat16)
        refs[-1][i * CAP : (i + 2) * CAP] = rows


def back_kernel(*refs):
    w_ref, out_ref, laid_ref = refs[4], refs[-2], refs[-1]
    quarter = refs[0].shape[0]
    for kind in range(2):
        for at in range(2):
            rows = refs[2 * kind + at][...]
            laid_ref[kind, 0, at * quarter : (at + 1) * quarter] = rows
    out_ref[0] = contract(laid_ref[0, 0], w_ref[...], ((1,), (1,)))


def update_kernel(
    h_own_ref, h_extra_ref, *refs
):
    c_refs = refs[:4]
    w_ref, m_ref, v_ref, out_ref = refs[4:]
    block, width = w_ref.shape
    half = c_refs[0].shape[2]
    depth = RUN * half
    total = jnp.zeros(w_ref.shape, jnp.float32)
    for kind, h_ref in enumerate((h_own_ref, h_extra_ref)):
        for at, part in enumerate((c_refs[kind][0], c_refs[2 + kind][0])):
            rows = h_ref[:, at * half : (at + 1) * half].reshape(depth, block)
            total += contract(rows, part.reshape(depth, width), ((0,), (0,)))
    m_new = beta_one * m_ref[...] + (1.0 - beta_one) * total
    v_new = beta_two * v_ref[...] + (1.0 - beta_two) * total * total
    direction = m_new / bias_one / (jnp.sqrt(v_new / bias_two) + epsilon)
    direction = direction + decay * w_ref[...].astype(jnp.float32)
    out_ref[...] = SCALE * direction


def take_kernel(row_ref, col_ref, want_ref, *refs):
    sel = jnp.where(choose(row_ref[0], col_ref[0], want_ref[...]), 1.0, 0.0).astype(jnp.bfloat16)
    part = ROWS // GRID
    rows = jnp.zeros(refs[-1].shape, jnp.float32)
    for step, ref in enumerate(refs[:-1]):
        rows += contract(sel[step * part : (step + 1) * part], ref[...], ((0,), (0,)))
    refs[-1][...] = rows.astype(jnp.bfloat16)


def in_hbm(value):
    return pltpu.with_memory_space_constraint(value, pltpu.HBM)


def params(limit):
    return pltpu.CompilerParams(vmem_limit_bytes=limit * MB)


def whole(shape):
    return pl.BlockSpec(shape, lambda *_: (0,) * len(shape))


def local(
    hidden_acts,
    out_grad,
    gate_probs,
    route,
    weights,
    first_moment,
    second_moment,
    old_slot,
    new_slot,
    partner,
):
    tokens, top, hidden = hidden_acts.shape
    count = tokens * top
    width = weights.shape[2]
    index = lax.axis_index("ep").astype(jnp.int32)
    y = index % RUN
    core = (lax.axis_index("dp") % 2).astype(jnp.int32)

    numbers = jnp.arange(GROUPS, dtype=jnp.int32)
    held = old_slot[None, :] == numbers[:, None]
    own = jnp.sum(jnp.where(held, numbers[None, :], 0), axis=1)
    mate = jnp.sum(jnp.where(held, partner[None, :], 0), axis=1)
    mate = jnp.where(mate == own, -1, mate)
    want = jnp.stack([own, mate]).astype(jnp.float32)
    steps = jnp.array([SHIFTS[0] + SHIFTS[1], SHIFTS[1] + SHIFTS[0]], jnp.int32)
    steps = jnp.where(core == 0, steps[0], steps[1])
    x, z = index // (GRID * RUN), index // RUN % GRID
    to = (x + steps[:HALF, 0]) % GRID * GRID + (z + steps[:HALF, 1]) % GRID
    by = (x - steps[:, 0]) % GRID * GRID + (z - steps[:, 1]) % GRID
    want_to = jnp.sum(jnp.where(to[:, None] == numbers[None, :], want[:, None, :], 0.0), axis=2)
    want_h = jnp.broadcast_to(want[:, :, None], (2, GROUPS, CAP)).reshape(2, ROWS, 1)
    outer, inner = numbers // GRID, numbers % GRID
    home = (x + outer) % GRID * GRID + (z + inner) % GRID
    owner = (x - inner) % GRID * GRID + (z - outer) % GRID
    want = jnp.sum(jnp.where(owner[:, None] == numbers[None, :], want[:1], 0.0), axis=1)
    want = jnp.broadcast_to(want[:, None], (GROUPS, CAP)).reshape(ROWS, 1)
    want_to = jnp.broadcast_to(want_to[:, :, None], (2, HALF, CAP)).reshape(2, ROWS // 2, 1)
    place = jnp.arange(CAP, dtype=jnp.int32)[None, :]
    home_to = (home[:, None] * CAP + place).reshape(ROWS, 1)
    home_from = (by[:, None] * CAP + place).reshape(1, ROWS)
    order_h = (by[:, None] * CAP + place).reshape(ROWS, 1)
    source = jnp.sum(
        jnp.where(new_slot[None, :] == numbers[:, None], old_slot[None, :], 0), axis=1
    )

    routes = route.astype(jnp.float32)
    packed = pl.pallas_call(
        pack_kernel,
        grid_spec=pltpu.PrefetchScalarGridSpec(
            num_scalar_prefetch=1,
            grid=(1,),
            in_specs=[whole((tokens, RUN * width)), whole((tokens, 2 * top))],
            out_specs=[whole((tokens, width + LANES))] * RUN,
        ),
        out_shape=[jax.ShapeDtypeStruct((tokens, width + LANES), jnp.bfloat16)] * RUN,
        compiler_params=params(8),
        name="pack",
    )(y.reshape(1), out_grad, jnp.concatenate([routes, gate_probs], axis=1))
    packed = [packed[0]] + [lax.ppermute(packed[s], "ep", along_y(s)) for s in range(1, RUN)]
    packed = jnp.stack(packed)

    own_row = routes.T.reshape(1, 1, count)
    own_col = own_row.reshape(1, count, 1)
    acts = hidden_acts.transpose(1, 0, 2).reshape(count, hidden)
    sent_h = pl.pallas_call(
        send_h_kernel,
        out_shape=jax.ShapeDtypeStruct((ROWS, 2 * hidden), jnp.bfloat16),
        compiler_params=params(8),
        name="send_h",
    )(own_row, own_col, want_h, acts)
    got_h = lax.all_to_all(sent_h, "ep", 0, 0, axis_index_groups=SAME_Y, tiled=True)

    send_c = pl.pallas_call(
        send_c_kernel,
        grid_spec=pltpu.PrefetchScalarGridSpec(
            num_scalar_prefetch=1,
            grid=(2, RUN),
            in_specs=[
                pl.BlockSpec((1, ROWS // 2, 1), lambda k, s, y: (k, 0, 0)),
                pl.BlockSpec(
                    (1, tokens, width + LANES), lambda k, s, y: ((y[0] + RUN - s) % RUN, 0, 0)
                ),
            ],
            out_specs=[pl.BlockSpec((CAP, width), lambda k, s, y: (0, RUN * k + s))] * HALF,
        ),
        out_shape=[pltpu.HBM((CAP, 2 * RUN * width), jnp.bfloat16)] * HALF,
        compiler_params=params(12),
        name="send_c",
    )(y.reshape(1), want_to, packed)
    send_c = list(send_c)
    got_h, send_c[0] = lax.optimization_barrier((got_h, send_c[0]))
    got_h = pl.pallas_call(
        order_kernel,
        out_shape=jax.ShapeDtypeStruct((ROWS, 2 * hidden), jnp.bfloat16),
        compiler_params=params(8),
        name="order_h",
    )(order_h, got_h)
    all_h = lax.all_gather(got_h, "ep", axis_index_groups=SAME_RUN, axis=0, tiled=False)
    got_c = [lax.ppermute(send_c[i], ("ep", "dp"), nearest(i)) for i in range(HALF)]
    own_c, mate_c = [], []
    for at in range(0, HALF, HALF // 2):
        own_c.append(
            pl.pallas_call(
                join_kernel,
                out_shape=jax.ShapeDtypeStruct((ROWS // 4, 2 * RUN * width), jnp.bfloat16),
                compiler_params=params(8),
                name="join",
            )(*got_c[at : at + HALF // 2])
        )
        mate_c.append(lax.ppermute(own_c[-1], "dp", OTHER_CORE))

    weight = weights[0]
    partial_back, laid = [], []
    for at, pair in enumerate((own_c, mate_c)):
        partial_back, rows = pl.pallas_call(
            back_kernel,
            grid=(RUN,),
            in_specs=[pl.BlockSpec((ROWS // 4, width), lambda s: (0, s))] * 2
            + [pl.BlockSpec((ROWS // 4, width), lambda s: (0, RUN + s))] * 2
            + [whole((hidden, width))]
            + [pl.BlockSpec(memory_space=pl.ANY)] * at,
            out_specs=[
                pl.BlockSpec((1, ROWS // 2, hidden), lambda s, at=at: (s, at, 0)),
                pl.BlockSpec((2, 1, ROWS // 2, width), lambda s: (0, s, 0, 0)),
            ],
            out_shape=[
                pltpu.HBM((RUN, ROWS, hidden), jnp.float32),
                pltpu.HBM((2, RUN, ROWS // 2, width), jnp.bfloat16),
            ],
            input_output_aliases={5: 0} if at else {},
            compiler_params=params(24),
            name="back",
        )(*pair, *pair, weight, *([partial_back] if at else []))
        laid.append(rows)
    summed = lax.psum_scatter(
        partial_back, "ep", scatter_dimension=0, axis_index_groups=SAME_RUN, tiled=False
    )
    part = jax.ShapeDtypeStruct((ROWS // GRID, hidden), jnp.bfloat16)
    back = pl.pallas_call(
        return_kernel, out_shape=[part] * GRID, compiler_params=params(8), name="return"
    )(home_to, home_from, in_hbm(summed))
    back = [back[0]] + [lax.ppermute(back[k], "ep", along_grid(k, 0)) for k in range(1, GRID)]
    back = pl.pallas_call(
        turn_kernel, out_shape=[part] * GRID, compiler_params=params(8), name="turn"
    )(*back)
    back = [back[0]] + [lax.ppermute(back[k], "ep", along_grid(0, k)) for k in range(1, GRID)]
    hidden_out = pl.pallas_call(
        take_kernel,
        out_shape=jax.ShapeDtypeStruct((count, hidden), jnp.bfloat16),
        compiler_params=params(8),
        name="take",
    )(own_row, own_col, want, *back)
    hidden_out = hidden_out.reshape(top, tokens, hidden).transpose(1, 0, 2)

    block = 128
    grid = hidden // block
    update = pl.pallas_call(
        update_kernel,
        grid=(grid,),
        in_specs=[
            pl.BlockSpec((RUN, ROWS, block), lambda i: (0, 0, i)),
            pl.BlockSpec((RUN, ROWS, block), lambda i: (0, 0, grid + i)),
        ]
        + [
            pl.BlockSpec((1, RUN, ROWS // 2, width), lambda i, k=k: (k, 0, 0, 0))
            for k in (0, 1, 0, 1)
        ]
        + [pl.BlockSpec((block, width), lambda i: (i, 0))] * 3,
        out_specs=pl.BlockSpec((block, width), lambda i: (i, 0)),
        out_shape=jax.ShapeDtypeStruct((hidden, width), jnp.float32),
        compiler_params=params(24),
        name="update",
    )(
        in_hbm(all_h),
        in_hbm(all_h),
        *[in_hbm(rows) for rows in laid for _ in range(2)],
        weight,
        in_hbm(first_moment[0]),
        in_hbm(second_moment[0]),
    )

    spread = update.astype(jnp.float16).reshape(GROUPS, hidden // GROUPS, width)
    spread = lax.all_to_all(spread, "ep", 0, 0, axis_index_groups=SAME_Y, tiled=True)
    placed = lax.all_to_all(spread[source], "ep", 0, 0, axis_index_groups=SAME_Y, tiled=True)
    placed = placed.reshape(1, hidden, width).astype(jnp.float32) * (1.0 / SCALE)
    return (hidden_out, placed)


def solution(mesh):
    return jax.shard_map(
        local,
        mesh=mesh,
        in_specs=(
            P("ep", None, "dp"),
            P("ep", None),
            P("ep", None),
            P("ep", None),
            P("ep", "dp", None),
            P("ep", "dp", None),
            P("ep", "dp", None),
            P(),
            P(),
            P(),
        ),
        out_specs=(P("ep", None, "dp"), P("ep", "dp", None)),
        check_vma=False,
    )
```

```python
import jax
import jax.numpy as jnp
from jax import lax
from jax.experimental import pallas as pl
from jax.experimental.pallas import tpu as pltpu
from jax.sharding import PartitionSpec as P

beta_one = 0.9
beta_two = 0.95
decay = 0.1
epsilon = 1e-08
bias_one = 1.0 - (0.9**50) ** 2
bias_two = 1.0 - (0.95**50) ** 2

RUN = 4
GROUPS = 16
CAP = 24
ROWS = GROUPS * CAP
SCALE = 2048.0
SAME_Y = [[g * RUN + y for g in range(GROUPS)] for y in range(RUN)]
SAME_RUN = [[g * RUN + y for y in range(RUN)] for g in range(GROUPS)]
OTHER_CORE = [(0, 1), (1, 0), (2, 3), (3, 2)]
GRID = 4
SHIFTS = [
    [(0, 0), (2, 2), (1, 2), (2, 1), (3, 3), (0, 3), (1, 0), (1, 1)],
    [(2, 0), (3, 2), (2, 3), (1, 3), (0, 2), (3, 1), (0, 1), (3, 0)],
]
HALF = GROUPS // 2
LANES = 128
MB = 1024 * 1024


def contract(a, b, dims):
    return lax.dot_general(a, b, ((dims[0], dims[1]), ((), ())), preferred_element_type=jnp.float32)


def order_of(index, tokens):
    return 2 * (index % tokens) + index // tokens


def choose(row, col, want):
    count = row.shape[1]
    tokens = count // 2
    lane = order_of(lax.broadcasted_iota(jnp.int32, (count, count), 1), tokens)
    line = order_of(lax.broadcasted_iota(jnp.int32, (count, count), 0), tokens)
    ahead = jnp.where((row == col) & (line < lane), 1.0, 0.0)
    position = jnp.sum(ahead, axis=0, keepdims=True)
    place = (lax.broadcasted_iota(jnp.int32, (want.shape[0], 1), 0) % CAP).astype(jnp.float32)
    return (row == want) & (position == place)


def along_y(step):
    return [(i, i // RUN * RUN + (i + step) % RUN) for i in range(GROUPS * RUN)]


def along_grid(step_x, step_z):
    pairs = []
    for i in range(GROUPS * RUN):
        x, z, y = i // (GRID * RUN), i // RUN % GRID, i % RUN
        pairs.append((i, ((x + step_x) % GRID * GRID + (z + step_z) % GRID) * RUN + y))
    return pairs


def nearest(number):
    pairs = []
    for i in range(GROUPS * RUN):
        x, z_low, y = i // (GRID * RUN), i // RUN % GRID, i % RUN
        for d in range(4):
            step_x, step_z = SHIFTS[d % 2][number]
            z = d // 2 * GRID + z_low
            step = (2 if z % 2 == 0 else -2) if step_z == 2 else (-1 if step_z == 3 else step_z)
            to_z = (z + step) % (2 * GRID)
            to = ((x + step_x) % GRID * GRID + to_z % GRID) * RUN + y
            pairs.append((i * 4 + d, to * 4 + to_z // GRID * 2 + d % 2))
    return pairs


def pack_kernel(y_ref, grad_ref, about_ref, *out_refs):
    width = grad_ref.shape[1] // RUN
    tokens = grad_ref.shape[0]
    about = about_ref[...]
    lane = lax.broadcasted_iota(jnp.int32, (tokens, LANES), 1)
    block = jnp.zeros((tokens, LANES), jnp.float32)
    place = 0
    for k in range(4):
        rest = about[:, k : k + 1]
        for _ in range(1 if k < 2 else 3):
            piece = rest.astype(jnp.bfloat16).astype(jnp.float32)
            block = jnp.where(lane == place, piece, block)
            rest = rest - piece
            place += 1
    for step, out_ref in enumerate(out_refs):
        quarter = (y_ref[0] + step) % RUN
        start = pl.multiple_of(quarter * width, LANES)
        out_ref[:, :width] = grad_ref[:, pl.ds(start, width)]
        out_ref[:, width:] = block.astype(jnp.bfloat16)


def send_h_kernel(row_ref, col_ref, want_ref, acts_ref, out_ref):
    width = acts_ref.shape[1]
    for kind in range(2):
        sel = choose(row_ref[0], col_ref[0], want_ref[kind])
        rows = contract(jnp.where(sel, 1.0, 0.0).astype(jnp.bfloat16), acts_ref[...], ((1,), (0,)))
        out_ref[:, kind * width : (kind + 1) * width] = rows.astype(jnp.bfloat16)


def send_c_kernel(y_ref, want_ref, packed_ref, *out_refs):
    tokens = packed_ref.shape[1]
    width = packed_ref.shape[2] - LANES
    block = packed_ref[0, :, width:]
    eye = lax.broadcasted_iota(jnp.int32, (tokens, tokens), 0) == lax.broadcasted_iota(
        jnp.int32, (tokens, tokens), 1
    )
    lines = contract(block, jnp.where(eye, 1.0, 0.0).astype(jnp.bfloat16), ((0,), (0,)))
    columns = block.astype(jnp.float32)
    row = jnp.concatenate([lines[0:1], lines[1:2]], axis=1)
    col = jnp.concatenate([columns[:, 0:1], columns[:, 1:2]], axis=0)
    gates = [lines[2 + 3 * k : 3 + 3 * k] + lines[3 + 3 * k : 4 + 3 * k] for k in range(2)]
    gates = [gates[k] + lines[4 + 3 * k : 5 + 3 * k] for k in range(2)]
    sel = choose(row, col, want_ref[0])
    gate = jnp.sum(
        jnp.where(sel, jnp.concatenate(gates, axis=1), 0.0), axis=1, keepdims=True
    )
    sel = jnp.where(sel, 1.0, 0.0)
    sel = (sel[:, :tokens] + sel[:, tokens:]).astype(jnp.bfloat16)
    rows = gate * contract(sel, packed_ref[0, :, :width], ((1,), (0,)))
    for i, out_ref in enumerate(out_refs):
        out_ref[...] = rows[i * CAP : (i + 1) * CAP].astype(jnp.bfloat16)


def order_kernel(order_ref, value_ref, out_ref):
    lane = lax.broadcasted_iota(jnp.int32, (ROWS, ROWS), 1)
    turn = jnp.where(lane == order_ref[...], 1.0, 0.0).astype(jnp.bfloat16)
    out_ref[...] = contract(turn, value_ref[...], ((1,), (0,))).astype(jnp.bfloat16)


def return_kernel(to_ref, from_ref, value_ref, *out_refs):
    turn = jnp.where(to_ref[...] == from_ref[...], 1.0, 0.0).astype(jnp.bfloat16)
    rows = contract(turn, value_ref[...].astype(jnp.bfloat16), ((1,), (0,))).astype(jnp.bfloat16)
    part = ROWS // GRID
    for step, out_ref in enumerate(out_refs):
        out_ref[...] = rows[step * part : (step + 1) * part]


def turn_kernel(*refs):
    values = [ref[...].astype(jnp.float32) for ref in refs[:GRID]]
    for step, out_ref in enumerate(refs[GRID:]):
        rows = [value[step * CAP : (step + 1) * CAP] for value in values]
        out_ref[...] = jnp.concatenate(rows, axis=0).astype(jnp.bfloat16)


def join_kernel(*refs):
    for i in range(0, len(refs) - 1, 2):
        pair = [ref[...].astype(jnp.float32) for ref in refs[i : i + 2]]
        rows = jnp.concatenate(pair, axis=0).astype(jnp.bfloat16)
        refs[-1][i * CAP : (i + 2) * CAP] = rows


def back_kernel(*refs):
    w_ref, out_ref, laid_ref = refs[4], refs[-2], refs[-1]
    quarter = refs[0].shape[0]
    sources, half, width = laid_ref.shape[1:]
    for kind in range(2):
        for at in range(2):
            for source in range(sources):
                rows = refs[2 * kind + at][:, source * width : (source + 1) * width]
                laid_ref[kind, source, at * quarter : (at + 1) * quarter] = rows
    rows = contract(laid_ref[0].reshape(sources * half, width), w_ref[...], ((1,), (1,)))
    out_ref[...] = rows.reshape(sources, half, rows.shape[1])


def update_kernel(
    h_own_ref, h_extra_ref, *refs
):
    c_refs = refs[:4]
    w_ref, m_ref, v_ref, out_ref = refs[4:]
    block, width = w_ref.shape
    half = c_refs[0].shape[2]
    depth = RUN * half
    total = jnp.zeros(w_ref.shape, jnp.float32)
    for kind, h_ref in enumerate((h_own_ref, h_extra_ref)):
        for at, part in enumerate((c_refs[kind][0], c_refs[2 + kind][0])):
            rows = h_ref[:, at * half : (at + 1) * half].reshape(depth, block)
            total += contract(rows, part.reshape(depth, width), ((0,), (0,)))
    m_new = beta_one * m_ref[...] + (1.0 - beta_one) * total
    v_new = beta_two * v_ref[...] + (1.0 - beta_two) * total * total
    direction = m_new / bias_one / (jnp.sqrt(v_new / bias_two) + epsilon)
    direction = direction + decay * w_ref[...].astype(jnp.float32)
    out_ref[...] = SCALE * direction


def take_kernel(row_ref, col_ref, want_ref, *refs):
    sel = jnp.where(choose(row_ref[0], col_ref[0], want_ref[...]), 1.0, 0.0).astype(jnp.bfloat16)
    part = ROWS // GRID
    rows = jnp.zeros(refs[-1].shape, jnp.float32)
    for step, ref in enumerate(refs[:-1]):
        rows += contract(sel[step * part : (step + 1) * part], ref[...], ((0,), (0,)))
    refs[-1][...] = rows.astype(jnp.bfloat16)


def in_hbm(value):
    return pltpu.with_memory_space_constraint(value, pltpu.HBM)


def params(limit):
    return pltpu.CompilerParams(vmem_limit_bytes=limit * MB)


def whole(shape):
    return pl.BlockSpec(shape, lambda *_: (0,) * len(shape))


def local(
    hidden_acts,
    out_grad,
    gate_probs,
    route,
    weights,
    first_moment,
    second_moment,
    old_slot,
    new_slot,
    partner,
):
    tokens, top, hidden = hidden_acts.shape
    count = tokens * top
    width = weights.shape[2]
    index = lax.axis_index("ep").astype(jnp.int32)
    y = index % RUN
    core = (lax.axis_index("dp") % 2).astype(jnp.int32)

    numbers = jnp.arange(GROUPS, dtype=jnp.int32)
    held = old_slot[None, :] == numbers[:, None]
    own = jnp.sum(jnp.where(held, numbers[None, :], 0), axis=1)
    mate = jnp.sum(jnp.where(held, partner[None, :], 0), axis=1)
    mate = jnp.where(mate == own, -1, mate)
    want = jnp.stack([own, mate]).astype(jnp.float32)
    steps = jnp.array([SHIFTS[0] + SHIFTS[1], SHIFTS[1] + SHIFTS[0]], jnp.int32)
    steps = jnp.where(core == 0, steps[0], steps[1])
    x, z = index // (GRID * RUN), index // RUN % GRID
    to = (x + steps[:HALF, 0]) % GRID * GRID + (z + steps[:HALF, 1]) % GRID
    by = (x - steps[:, 0]) % GRID * GRID + (z - steps[:, 1]) % GRID
    want_to = jnp.sum(jnp.where(to[:, None] == numbers[None, :], want[:, None, :], 0.0), axis=2)
    want_h = jnp.broadcast_to(want[:, :, None], (2, GROUPS, CAP)).reshape(2, ROWS, 1)
    outer, inner = numbers // GRID, numbers % GRID
    home = (x + outer) % GRID * GRID + (z + inner) % GRID
    owner = (x - inner) % GRID * GRID + (z - outer) % GRID
    want = jnp.sum(jnp.where(owner[:, None] == numbers[None, :], want[:1], 0.0), axis=1)
    want = jnp.broadcast_to(want[:, None], (GROUPS, CAP)).reshape(ROWS, 1)
    want_to = jnp.broadcast_to(want_to[:, :, None], (2, HALF, CAP)).reshape(2, ROWS // 2, 1)
    place = jnp.arange(CAP, dtype=jnp.int32)[None, :]
    home_to = (home[:, None] * CAP + place).reshape(ROWS, 1)
    home_from = (by[:, None] * CAP + place).reshape(1, ROWS)
    order_h = (by[:, None] * CAP + place).reshape(ROWS, 1)
    source = jnp.sum(
        jnp.where(new_slot[None, :] == numbers[:, None], old_slot[None, :], 0), axis=1
    )

    routes = route.astype(jnp.float32)
    packed = pl.pallas_call(
        pack_kernel,
        grid_spec=pltpu.PrefetchScalarGridSpec(
            num_scalar_prefetch=1,
            grid=(1,),
            in_specs=[whole((tokens, RUN * width)), whole((tokens, 2 * top))],
            out_specs=[whole((tokens, width + LANES))] * RUN,
        ),
        out_shape=[jax.ShapeDtypeStruct((tokens, width + LANES), jnp.bfloat16)] * RUN,
        compiler_params=params(8),
        name="pack",
    )(y.reshape(1), out_grad, jnp.concatenate([routes, gate_probs], axis=1))
    packed = [packed[0]] + [lax.ppermute(packed[s], "ep", along_y(s)) for s in range(1, RUN)]
    packed = jnp.stack(packed)

    own_row = routes.T.reshape(1, 1, count)
    own_col = own_row.reshape(1, count, 1)
    acts = hidden_acts.transpose(1, 0, 2).reshape(count, hidden)
    sent_h = pl.pallas_call(
        send_h_kernel,
        out_shape=jax.ShapeDtypeStruct((ROWS, 2 * hidden), jnp.bfloat16),
        compiler_params=params(8),
        name="send_h",
    )(own_row, own_col, want_h, acts)
    got_h = lax.all_to_all(sent_h, "ep", 0, 0, axis_index_groups=SAME_Y, tiled=True)

    send_c = pl.pallas_call(
        send_c_kernel,
        grid_spec=pltpu.PrefetchScalarGridSpec(
            num_scalar_prefetch=1,
            grid=(2, RUN),
            in_specs=[
                pl.BlockSpec((1, ROWS // 2, 1), lambda k, s, y: (k, 0, 0)),
                pl.BlockSpec(
                    (1, tokens, width + LANES), lambda k, s, y: ((y[0] + RUN - s) % RUN, 0, 0)
                ),
            ],
            out_specs=[pl.BlockSpec((CAP, width), lambda k, s, y: (0, RUN * k + s))] * HALF,
        ),
        out_shape=[pltpu.HBM((CAP, 2 * RUN * width), jnp.bfloat16)] * HALF,
        compiler_params=params(12),
        name="send_c",
    )(y.reshape(1), want_to, packed)
    send_c = list(send_c)
    got_h, send_c[0] = lax.optimization_barrier((got_h, send_c[0]))
    got_h = pl.pallas_call(
        order_kernel,
        out_shape=jax.ShapeDtypeStruct((ROWS, 2 * hidden), jnp.bfloat16),
        compiler_params=params(8),
        name="order_h",
    )(order_h, got_h)
    all_h = lax.all_gather(got_h, "ep", axis_index_groups=SAME_RUN, axis=0, tiled=False)
    got_c = [lax.ppermute(send_c[i], ("ep", "dp"), nearest(i)) for i in range(HALF)]
    own_c, mate_c = [], []
    for at in range(0, HALF, HALF // 2):
        own_c.append(
            pl.pallas_call(
                join_kernel,
                out_shape=jax.ShapeDtypeStruct((ROWS // 4, 2 * RUN * width), jnp.bfloat16),
                compiler_params=params(8),
                name="join",
            )(*got_c[at : at + HALF // 2])
        )
        mate_c.append(lax.ppermute(own_c[-1], "dp", OTHER_CORE))

    weight = weights[0]
    partial_back, laid = [], []
    for at, pair in enumerate((own_c, mate_c)):
        partial_back, rows = pl.pallas_call(
            back_kernel,
            grid=(2,),
            in_specs=[pl.BlockSpec((ROWS // 4, 2 * width), lambda s: (0, s))] * 2
            + [pl.BlockSpec((ROWS // 4, 2 * width), lambda s: (0, 2 + s))] * 2
            + [whole((hidden, width))]
            + [pl.BlockSpec(memory_space=pl.ANY)] * at,
            out_specs=[
                pl.BlockSpec((2, ROWS // 2, hidden), lambda s, at=at: (s, at, 0)),
                pl.BlockSpec((2, 2, ROWS // 2, width), lambda s: (0, s, 0, 0)),
            ],
            out_shape=[
                pltpu.HBM((RUN, ROWS, hidden), jnp.float32),
                pltpu.HBM((2, RUN, ROWS // 2, width), jnp.bfloat16),
            ],
            input_output_aliases={5: 0} if at else {},
            compiler_params=params(24),
            name="back",
        )(*pair, *pair, weight, *([partial_back] if at else []))
        laid.append(rows)
    summed = lax.psum_scatter(
        partial_back, "ep", scatter_dimension=0, axis_index_groups=SAME_RUN, tiled=False
    )
    part = jax.ShapeDtypeStruct((ROWS // GRID, hidden), jnp.bfloat16)
    back = pl.pallas_call(
        return_kernel, out_shape=[part] * GRID, compiler_params=params(8), name="return"
    )(home_to, home_from, in_hbm(summed))
    back = [back[0]] + [lax.ppermute(back[k], "ep", along_grid(k, 0)) for k in range(1, GRID)]
    back = pl.pallas_call(
        turn_kernel, out_shape=[part] * GRID, compiler_params=params(8), name="turn"
    )(*back)
    back = [back[0]] + [lax.ppermute(back[k], "ep", along_grid(0, k)) for k in range(1, GRID)]
    hidden_out = pl.pallas_call(
        take_kernel,
        out_shape=jax.ShapeDtypeStruct((count, hidden), jnp.bfloat16),
        compiler_params=params(8),
        name="take",
    )(own_row, own_col, want, *back)
    hidden_out = hidden_out.reshape(top, tokens, hidden).transpose(1, 0, 2)

    block = 128
    grid = hidden // block
    update = pl.pallas_call(
        update_kernel,
        grid=(grid,),
        in_specs=[
            pl.BlockSpec((RUN, ROWS, block), lambda i: (0, 0, i)),
            pl.BlockSpec((RUN, ROWS, block), lambda i: (0, 0, grid + i)),
        ]
        + [
            pl.BlockSpec((1, RUN, ROWS // 2, width), lambda i, k=k: (k, 0, 0, 0))
            for k in (0, 1, 0, 1)
        ]
        + [pl.BlockSpec((block, width), lambda i: (i, 0))] * 3,
        out_specs=pl.BlockSpec((block, width), lambda i: (i, 0)),
        out_shape=jax.ShapeDtypeStruct((hidden, width), jnp.float32),
        compiler_params=params(24),
        name="update",
    )(
        in_hbm(all_h),
        in_hbm(all_h),
        *[in_hbm(rows) for rows in laid for _ in range(2)],
        weight,
        in_hbm(first_moment[0]),
        in_hbm(second_moment[0]),
    )

    spread = update.astype(jnp.float16).reshape(GROUPS, hidden // GROUPS, width)
    spread = lax.all_to_all(spread, "ep", 0, 0, axis_index_groups=SAME_Y, tiled=True)
    placed = lax.all_to_all(spread[source], "ep", 0, 0, axis_index_groups=SAME_Y, tiled=True)
    placed = placed.reshape(1, hidden, width).astype(jnp.float32) * (1.0 / SCALE)
    return (hidden_out, placed)


def solution(mesh):
    return jax.shard_map(
        local,
        mesh=mesh,
        in_specs=(
            P("ep", None, "dp"),
            P("ep", None),
            P("ep", None),
            P("ep", None),
            P("ep", "dp", None),
            P("ep", "dp", None),
            P("ep", "dp", None),
            P(),
            P(),
            P(),
        ),
        out_specs=(P("ep", None, "dp"), P("ep", "dp", None)),
        check_vma=False,
    )
```
